32 devices in a mesh: gx: 8 (over z, core), yz: 4 (over y, x).
Axes of the slice: x: 2, y: 2, z: 4, core: 2. Of those that a mesh axis runs over, the one named last changes fastest.
Arguments:
- state: float32 [5, 128, 64, 256], P(None, 'gx', 'yz'), may hold values from -3 to 9, as said below
- register: float32 [5, 128, 64, 256], P(None, 'gx', 'yz'), may hold values from -4 to 4
Outputs:
- register_out: float32 [5, 128, 64, 256], P(None, 'gx', 'yz')
- filtered: float32 [5, 128, 64, 256], P(None, 'gx', 'yz')
The draws below stay inside these ranges and needn't reach their ends.
Inputs may be any that keep to these rules, and one draw needn't show every extreme that they name: state holds the density, the three momenta and the total energy of an ideal gas with ratio of specific heats 1.4; in every cell the density lies between 0.4 and 2.2 and the pressure between 0.4 and 2.1.
All inputs are finite; a program needn't handle non-finite values.
Results may differ from the reference program's by a relative error of at most 0.0003.
Values sent between devices are 32-bit elements; how exact they have to be, the bound alone decides.
A program may use at most 128 MiB of HBM per device.

```python
import jax
import jax.numpy as jnp

NZ = 256
NX = 128
NY = 64


def draw_state(key, part):
    keys = jax.random.split(key, 3)
    shape = (NX, NY, NZ)
    coord_x = (2.0 * jnp.pi / NX * jnp.arange(NX, dtype=jnp.float32))[:, None, None]
    coord_y = (2.0 * jnp.pi / NY * jnp.arange(NY, dtype=jnp.float32))[None, :, None]
    coord_z = (2.0 * jnp.pi / NZ * jnp.arange(NZ, dtype=jnp.float32))[None, None, :]
    waves = jnp.cos(2.0 * coord_x) + jnp.cos(2.0 * coord_y)
    density = jnp.exp(jax.random.uniform(keys[0], shape, jnp.float32, -0.5, 0.5))
    rough = 0.25 * jax.random.truncated_normal(keys[1], -3.0, 3.0, (3,) + shape, jnp.float32)
    swirl = 0.5
    pressure = jnp.exp(jax.random.uniform(keys[2], shape, jnp.float32, -0.5, 0.5)) * (1.0 + 0.1 * waves)
    speed_x = swirl * jnp.sin(coord_x) * jnp.cos(coord_y) * jnp.cos(coord_z) + rough[0]
    speed_y = -swirl * jnp.cos(coord_x) * jnp.sin(coord_y) * jnp.cos(coord_z) + rough[1]
    speed_z = rough[2]
    energy = pressure / 0.4 + 0.5 * density * (speed_x * speed_x + speed_y * speed_y + speed_z * speed_z)
    return jnp.stack([density, density * speed_x, density * speed_y, density * speed_z, energy]).astype(jnp.float32)


def level_of(own_key, dims, pieces, least, largest):
    loudness, own = 1.0, jax.random.fold_in(own_key, 6)
    for position, shards_of in pieces:
        steps = jnp.exp(jax.random.uniform(jax.random.fold_in(own, position), (shards_of,), jnp.float32, least / len(pieces), largest / len(pieces)))
        loudness = loudness * jnp.repeat(steps, dims[position] // shards_of).reshape([-1 if axis == position else 1 for axis in range(len(dims))])
    return loudness


def noise(key, dims, spread, limit, cuts=(), kind=jnp.bfloat16):
    entries = spread * jax.random.normal(key, dims, jnp.float32)
    if cuts:
        entries = entries * level_of(key, dims, cuts, -0.22, 0.18)
    return jnp.clip(entries, -limit, limit).astype(kind)


def setup_inputs(seed: int = 0) -> dict:
    streams_of = jax.random.split(jax.random.key(seed), 3)
    return {
        "state": draw_state(jax.random.fold_in(streams_of[2], 71), 0),
        "register": noise(streams_of[1], (5, NX, NY, NZ), 0.3, 4.0, ((1, 8), (2, 4)), jnp.float32),
    }


gamma_gas = 1.4
central_weights = (4.0 / 5.0, -1.0 / 5.0, 4.0 / 105.0, -1.0 / 280.0)
filter_alpha = 0.49
register_decay = -5.0 / 9.0
register_gain = 15.0 / 16.0
time_step = 0.2


def primitives(fields):
    density = fields[0]
    speed_x = fields[1] / density
    speed_y = fields[2] / density
    speed_z = fields[3] / density
    kinetic = 0.5 * density * (speed_x * speed_x + speed_y * speed_y + speed_z * speed_z)
    pressure = (gamma_gas - 1.0) * (fields[4] - kinetic)
    enthalpy = (fields[4] + pressure) / density
    return (density, speed_x, speed_y, speed_z, pressure, enthalpy)


def pair_flux(left, right, direction):
    means = [0.5 * (one + other) for one, other in zip(left, right)]
    density, speed_x, speed_y, speed_z, pressure, enthalpy = means
    normal = (speed_x, speed_y, speed_z)[direction]
    mass = density * normal
    moment = [mass * speed_x, mass * speed_y, mass * speed_z]
    moment[direction] = moment[direction] + pressure
    return [mass] + moment + [mass * enthalpy]


def residual_of(state):
    prims = primitives(state)
    total = [jnp.zeros_like(state[0]) for field in range(5)]
    for direction in range(3):
        for offset in range(1, 5):
            weight = central_weights[offset - 1]
            ahead = tuple(jnp.roll(column, -offset, axis=direction) for column in prims)
            flux = pair_flux(prims, ahead, direction)
            total = [part - 2.0 * weight * (value - jnp.roll(value, offset, axis=direction)) for part, value in zip(total, flux)]
    return jnp.stack(total)


def reference(state, register):
    residual = residual_of(state)
    register_out = register_decay * register + time_step * residual
    section = state + register_gain * register_out
    alpha = filter_alpha
    coeffs = ((11.0 + 10.0 * alpha) / 16.0, (15.0 + 34.0 * alpha) / 32.0, (-3.0 + 6.0 * alpha) / 16.0, (1.0 - 2.0 * alpha) / 32.0)
    rhs = coeffs[0] * section
    for shift in range(1, 4):
        rhs = rhs + (coeffs[shift] / 2.0) * (jnp.roll(section, -shift, axis=1) + jnp.roll(section, shift, axis=1))
    waves = jnp.arange(NX // 2 + 1, dtype=jnp.float32)
    eigen = 1.0 + 2.0 * alpha * jnp.cos((2.0 * jnp.pi / NX) * waves)
    spectrum = jnp.fft.rfft(rhs, axis=1)
    filtered = jnp.fft.irfft(spectrum / eigen[None, :, None, None], n=NX, axis=1)
    return register_out, filtered.astype(jnp.float32)
```

```python
import functools

import jax
import jax.numpy as jnp
from jax import lax
from jax.experimental import pallas as pl
from jax.experimental.pallas import tpu as pltpu
from jax.sharding import PartitionSpec as P

gamma_gas = 1.4
central_weights = (4.0 / 5.0, -1.0 / 5.0, 4.0 / 105.0, -1.0 / 280.0)
filter_alpha = 0.49
register_decay = -5.0 / 9.0
register_gain = 15.0 / 16.0
time_step = 0.2
MESH = pl.DeviceIdType.MESH
LANES = 128
ROWS = 8


def filter_constants():
    alpha = filter_alpha
    a0 = (11.0 + 10.0 * alpha) / 16.0
    a1 = (15.0 + 34.0 * alpha) / 32.0
    a2 = (-3.0 + 6.0 * alpha) / 16.0
    a3 = (1.0 - 2.0 * alpha) / 32.0
    q2 = 4.0 * a3 / (2.0 * alpha)
    q1 = (2.0 * a2 - q2) / (2.0 * alpha)
    q0 = (a1 - 3.0 * a3 - q1) / (2.0 * alpha)
    rest = a0 - a2 - q0
    mu = (-1.0 + (1.0 - 4.0 * alpha * alpha) ** 0.5) / (2.0 * alpha)
    kappa = (1.0 + mu * mu) / (1.0 - mu * mu)
    return (q0 + 0.5 * q2, 0.5 * q1, 0.25 * q2), kappa * rest, mu


def primitives(fields):
    density = fields[0]
    inverse = 1.0 / density
    speeds = [fields[i] * inverse for i in (1, 2, 3)]
    kinetic = 0.5 * (
        fields[1] * speeds[0] + fields[2] * speeds[1] + fields[3] * speeds[2]
    )
    pressure = (gamma_gas - 1.0) * (fields[4] - kinetic)
    enthalpy = (fields[4] + pressure) * (0.5 * inverse)
    return [density] + [0.5 * speed for speed in speeds] + [pressure, enthalpy]


def pair_flux(left, right, direction, weight):
    density, speed_x, speed_y, speed_z, pressure, enthalpy = [
        one + other for one, other in zip(left, right)
    ]
    normal = (speed_x, speed_y, speed_z)[direction]
    mass = (weight * density) * normal
    moment = [mass * speed_x, mass * speed_y, mass * speed_z]
    moment[direction] = moment[direction] + weight * pressure
    return [mass] + moment + [mass * enthalpy]


def kernel(
    n_gx,
    n_yz,
    state,
    register,
    out_register,
    out_filtered,
    reg,
    prims,
    acc,
    xrecv,
    ysend,
    yrecv,
    sec,
    regout,
    filt,
    srecv,
    ab,
    pab,
    chip,
    chips,
    inc,
    pinc,
    xs,
    xr,
    ys,
    yr,
    ss,
    sr,
    abs_,
    abr,
    cs,
    cr,
    ins,
    inr,
    local,
):
    nf, nx, ny, nz = state.shape
    n_ch = nz // LANES
    tiles = ny // ROWS
    zs = n_gx // 2
    me = lax.axis_index("gx")
    mine = lax.axis_index("yz")
    core = lax.rem(me, 2)
    chip_at = lax.div(me, 2)
    nxt = lax.rem(me + 1, n_gx)
    prv = lax.rem(me + n_gx - 1, n_gx)
    partner = me + 1 - 2 * core
    ynxt = lax.rem(mine + 1, n_yz)
    yprv = lax.rem(mine + n_yz - 1, n_yz)

    def chip_peer(d):
        return 2 * lax.rem(chip_at + (1 - 2 * core) * d + zs, zs) + core

    barrier = pltpu.get_barrier_semaphore()
    peers = [(prv, mine), (nxt, mine), (me, yprv), (me, ynxt)]
    peers += [(chip_peer(d), mine) for d in range(1, zs)]
    for peer in peers:
        pl.semaphore_signal(barrier, inc=1, device_id=peer, device_id_type=MESH)

    get_register = pltpu.make_async_copy(register, reg, local.at[0])
    get_register.start()

    @pl.loop(0, nx)
    def _(x):
        for ch in range(n_ch):
            cols = pl.ds(ch * LANES, LANES)
            for f in range(nf):
                ysend[ch, 0, f, x] = state[f, x, pl.ds(0, ROWS), cols][:4]
                ysend[ch, 1, f, x] = state[f, x, pl.ds(ny - ROWS, ROWS), cols][4:]

    pl.semaphore_wait(barrier, len(peers))

    def remote(src, dst, send, recv, peer):
        return pltpu.make_async_remote_copy(
            src_ref=src,
            dst_ref=dst,
            send_sem=send,
            recv_sem=recv,
            device_id=peer,
            device_id_type=MESH,
        )

    def y_copies(ch):
        return [
            remote(
                ysend.at[ch, side],
                yrecv.at[ch, side],
                ys.at[ch, side],
                yr.at[ch, side],
                (me, (yprv, ynxt)[side]),
            )
            for side in range(2)
        ]

    ycopies = [y_copies(ch) for ch in range(n_ch)]
    xcopies = [
        remote(state.at[:, pl.ds(0, 4)], xrecv.at[0], xs.at[0], xr.at[0], (prv, mine)),
        remote(state.at[:, pl.ds(nx - 4, 4)], xrecv.at[1], xs.at[1], xr.at[1], (nxt, mine)),
    ]
    for copy in ycopies[0] + xcopies:
        copy.start()
    for ch in range(1, n_ch):
        for copy in ycopies[ch]:
            copy.start()

    weights = [-time_step * w for w in central_weights]

    @pl.loop(0, nx * tiles)
    def _(i):
        x = i // tiles
        rows = pl.ds(pl.multiple_of((i % tiles) * ROWS, ROWS), ROWS)
        own = primitives([state[f, x, rows, :] for f in range(nf)])
        for f in range(6):
            prims[f, x + 4, rows, :] = own[f]
        total = [jnp.zeros((ROWS, nz), jnp.float32) for _ in range(nf)]
        for l in range(1, 5):
            ahead = [pltpu.roll(q, nz - l, axis=1) for q in own]
            flux = pair_flux(own, ahead, 2, weights[l - 1])
            total = [t + (v - pltpu.roll(v, l, axis=1)) for t, v in zip(total, flux)]
        for f in range(nf):
            acc[f, x, rows, :] = total[f]

    for copy in xcopies:
        copy.wait_recv()

    @pl.loop(0, 4 * tiles)
    def _(i):
        x = i // tiles
        rows = pl.ds(pl.multiple_of((i % tiles) * ROWS, ROWS), ROWS)
        for side in range(2):
            got = primitives([xrecv[side, f, x, rows, :] for f in range(nf)])
            for f in range(6):
                prims[f, x + (nx + 4, 0)[side], rows, :] = got[f]

    @pl.loop(0, nx * tiles)
    def _(i):
        x = i // tiles
        rows = pl.ds(pl.multiple_of((i % tiles) * ROWS, ROWS), ROWS)
        for ch in range(n_ch):
            cols = pl.ds(ch * LANES, LANES)
            own = [prims[f, x + 4, rows, cols] for f in range(6)]
            total = [acc[f, x, rows, cols] for f in range(nf)]
            for l in range(1, 5):
                ahead = [prims[f, x + 4 + l, rows, cols] for f in range(6)]
                behind = [prims[f, x + 4 - l, rows, cols] for f in range(6)]
                up = pair_flux(own, ahead, 0, weights[l - 1])
                down = pair_flux(behind, own, 0, weights[l - 1])
                total = [t + (u - d) for t, u, d in zip(total, up, down)]
            for f in range(nf):
                acc[f, x, rows, cols] = total[f]

    get_register.wait()

    stencil, remainder, mu = filter_constants()
    rho = mu**nx
    span = ny + ROWS

    def section_of(ch):
        cols = pl.ds(ch * LANES, LANES)
        for copy in ycopies[ch]:
            copy.wait_recv()

        @pl.loop(0, nx)
        def _(x):
            halo = primitives(
                [
                    jnp.concatenate([yrecv[ch, 0, f, x], yrecv[ch, 1, f, x]], axis=0)
                    for f in range(nf)
                ]
            )
            own = [
                jnp.concatenate([prims[f, x + 4, :, cols], halo[f]], axis=0) for f in range(6)
            ]
            total = [jnp.zeros((ny, LANES), jnp.float32) for _ in range(nf)]
            for l in range(1, 5):
                ahead = [pltpu.roll(q, span - l, axis=0) for q in own]
                flux = pair_flux(own, ahead, 1, weights[l - 1])
                total = [
                    t + (v[:ny] - pltpu.roll(v, l, axis=0)[:ny]) for t, v in zip(total, flux)
                ]
            for f in range(nf):
                new = register_decay * reg[f, x, :, cols] + (acc[f, x, :, cols] + total[f])
                regout[ch, f, x] = new
                sec[ch, f, x] = state[f, x, :, cols] + register_gain * new

        @pl.loop(0, nf)
        def _(f):
            ahead = sec[ch, f, 0]
            back = sec[ch, f, nx - 1]
            for j in range(1, nx):
                ahead = sec[ch, f, j] + mu * ahead
                back = sec[ch, f, nx - 1 - j] + mu * back
            ab[ch, 0, f] = ahead
            ab[ch, 1, f] = back

    def section_copies(ch):
        return [
            remote(
                sec.at[ch, :, pl.ds(0, 2)],
                srecv.at[ch, 0],
                ss.at[ch, 0],
                sr.at[ch, 0],
                (prv, mine),
            ),
            remote(
                sec.at[ch, :, pl.ds(nx - 2, 2)],
                srecv.at[ch, 1],
                ss.at[ch, 1],
                sr.at[ch, 1],
                (nxt, mine),
            ),
        ]

    def ab_copy(ch):
        return remote(ab.at[ch], pab.at[ch], abs_.at[ch], abr.at[ch], (partner, mine))

    def chip_copies(ch):
        return [
            remote(
                chip.at[ch],
                chips.at[ch, d - 1],
                cs.at[ch, d - 1],
                cr.at[ch, d - 1],
                (chip_peer(d), mine),
            )
            for d in range(1, zs)
        ]

    def inc_copy(ch):
        return remote(inc.at[ch, core], pinc.at[ch], ins.at[ch], inr.at[ch], (partner, mine))

    scopies = [section_copies(ch) for ch in range(n_ch)]
    abcopies = [ab_copy(ch) for ch in range(n_ch)]
    ccopies = [chip_copies(ch) for ch in range(n_ch)]
    icopies = [inc_copy(ch) for ch in range(n_ch)]
    regcopies = [
        pltpu.make_async_copy(
            regout.at[ch],
            out_register.at[:, :, :, pl.ds(ch * LANES, LANES)],
            local.at[1 + ch],
        )
        for ch in range(n_ch)
    ]
    fcopies = [
        pltpu.make_async_copy(
            filt.at[ch],
            out_filtered.at[:, :, :, pl.ds(ch * LANES, LANES)],
            local.at[1 + n_ch + ch],
        )
        for ch in range(n_ch)
    ]

    def begin(ch):
        section_of(ch)
        abcopies[ch].start()
        for copy in scopies[ch]:
            copy.start()
        regcopies[ch].start()

    def across(ch):
        abcopies[ch].wait_recv()
        for f in range(nf):
            chip[ch, f] = pab[ch, core, f] + rho * ab[ch, core, f]
        for copy in ccopies[ch]:
            copy.start()

    def incoming(ch):
        for copy in ccopies[ch]:
            copy.wait_recv()
        scale = 1.0 / (1.0 - rho ** (2 * zs))
        for f in range(nf):
            total = (scale * rho ** (2 * (zs - 1))) * chip[ch, f]
            for d in range(1, zs):
                total = total + (scale * rho ** (2 * (d - 1))) * chips[ch, d - 1, f]
            inc[ch, core, f] = total
        icopies[ch].start()

    def finish(ch):
        icopies[ch].wait()
        for f in range(nf):
            inc[ch, 1 - core, f] = pab[ch, 1 - core, f] + rho * pinc[ch, f]
        for copy in scopies[ch]:
            copy.wait()

        @pl.loop(0, nf)
        def _(f):
            s = (
                [srecv[ch, 1, f, 0], srecv[ch, 1, f, 1]]
                + [sec[ch, f, j] for j in range(nx)]
                + [srecv[ch, 0, f, 0], srecv[ch, 0, f, 1]]
            )
            left = inc[ch, 0, f]
            for j in range(nx):
                left = s[j + 2] + mu * left
                near = (
                    stencil[0] * s[j + 2]
                    + stencil[1] * (s[j + 1] + s[j + 3])
                    + stencil[2] * (s[j] + s[j + 4])
                )
                filt[ch, f, j] = near + remainder * left
            right = inc[ch, 1, f]
            for j in reversed(range(nx)):
                filt[ch, f, j] = filt[ch, f, j] + (remainder * mu) * right
                right = s[j + 2] + mu * right

        fcopies[ch].start()

    for ch in range(n_ch):
        begin(ch)
        across(ch)
        if ch >= 1:
            incoming(ch - 1)
            finish(ch - 1)
    incoming(n_ch - 1)
    finish(n_ch - 1)

    for ch in range(n_ch):
        for copy in ycopies[ch]:
            copy.wait_send()
        abcopies[ch].wait_send()
        for copy in ccopies[ch]:
            copy.wait_send()
        regcopies[ch].wait()
        fcopies[ch].wait()
    for copy in xcopies:
        copy.wait_send()


def body(n_gx, n_yz, state, register):
    nf, nx, ny, nz = state.shape
    n_ch = nz // LANES
    zs = n_gx // 2
    f32 = jnp.float32
    dma = pltpu.SemaphoreType.DMA
    return pl.pallas_call(
        functools.partial(kernel, n_gx, n_yz),
        out_shape=[jax.ShapeDtypeStruct(state.shape, f32)] * 2,
        in_specs=[
            pl.BlockSpec(memory_space=pltpu.VMEM),
            pl.BlockSpec(memory_space=pl.ANY),
        ],
        out_specs=[pl.BlockSpec(memory_space=pl.ANY)] * 2,
        scratch_shapes=[
            pltpu.VMEM((nf, nx, ny, nz), f32),
            pltpu.VMEM((6, nx + 8, ny, nz), f32),
            pltpu.VMEM((nf, nx, ny, nz), f32),
            pltpu.VMEM((2, nf, 4, ny, nz), f32),
            pltpu.VMEM((n_ch, 2, nf, nx, 4, LANES), f32),
            pltpu.VMEM((n_ch, 2, nf, nx, 4, LANES), f32),
            pltpu.VMEM((n_ch, nf, nx, ny, LANES), f32),
            pltpu.VMEM((n_ch, nf, nx, ny, LANES), f32),
            pltpu.VMEM((n_ch, nf, nx, ny, LANES), f32),
            pltpu.VMEM((n_ch, 2, nf, 2, ny, LANES), f32),
            pltpu.VMEM((n_ch, 2, nf, ny, LANES), f32),
            pltpu.VMEM((n_ch, 2, nf, ny, LANES), f32),
            pltpu.VMEM((n_ch, nf, ny, LANES), f32),
            pltpu.VMEM((n_ch, zs - 1, nf, ny, LANES), f32),
            pltpu.VMEM((n_ch, 2, nf, ny, LANES), f32),
            pltpu.VMEM((n_ch, nf, ny, LANES), f32),
            dma((2,)),
            dma((2,)),
            dma((n_ch, 2)),
            dma((n_ch, 2)),
            dma((n_ch, 2)),
            dma((n_ch, 2)),
            dma((n_ch,)),
            dma((n_ch,)),
            dma((n_ch, zs - 1)),
            dma((n_ch, zs - 1)),
            dma((n_ch,)),
            dma((n_ch,)),
            dma((1 + 2 * n_ch,)),
        ],
        compiler_params=pltpu.CompilerParams(
            collective_id=0, has_side_effects=True, vmem_limit_bytes=40 * 1024 * 1024
        ),
    )(state, register)


def solution(mesh):
    spec = P(None, "gx", "yz", None)
    run = functools.partial(body, mesh.shape["gx"], mesh.shape["yz"])
    return jax.shard_map(
        lambda state, register: tuple(run(state, register)),
        mesh=mesh,
        in_specs=(spec, spec),
        out_specs=(spec, spec),
        check_vma=False,
    )
```

```python
import functools

import jax
import jax.numpy as jnp
from jax import lax
from jax.experimental import pallas as pl
from jax.experimental.pallas import tpu as pltpu
from jax.sharding import PartitionSpec as P

gamma_gas = 1.4
central_weights = (4.0 / 5.0, -1.0 / 5.0, 4.0 / 105.0, -1.0 / 280.0)
filter_alpha = 0.49
register_decay = -5.0 / 9.0
register_gain = 15.0 / 16.0
time_step = 0.2
MESH = pl.DeviceIdType.MESH
LANES = 128
ROWS = 8


def filter_constants():
    alpha = filter_alpha
    a0 = (11.0 + 10.0 * alpha) / 16.0
    a1 = (15.0 + 34.0 * alpha) / 32.0
    a2 = (-3.0 + 6.0 * alpha) / 16.0
    a3 = (1.0 - 2.0 * alpha) / 32.0
    q2 = 4.0 * a3 / (2.0 * alpha)
    q1 = (2.0 * a2 - q2) / (2.0 * alpha)
    q0 = (a1 - 3.0 * a3 - q1) / (2.0 * alpha)
    rest = a0 - a2 - q0
    mu = (-1.0 + (1.0 - 4.0 * alpha * alpha) ** 0.5) / (2.0 * alpha)
    kappa = (1.0 + mu * mu) / (1.0 - mu * mu)
    return (q0 + 0.5 * q2, 0.5 * q1, 0.25 * q2), kappa * rest, mu


def primitives(fields):
    density = fields[0]
    inverse = 1.0 / density
    speeds = [fields[i] * inverse for i in (1, 2, 3)]
    kinetic = 0.5 * (
        fields[1] * speeds[0] + fields[2] * speeds[1] + fields[3] * speeds[2]
    )
    pressure = (gamma_gas - 1.0) * (fields[4] - kinetic)
    enthalpy = (fields[4] + pressure) * (0.5 * inverse)
    return [density] + [0.5 * speed for speed in speeds] + [pressure, enthalpy]


def pair_flux(left, right, direction, weight):
    density, speed_x, speed_y, speed_z, pressure, enthalpy = [
        one + other for one, other in zip(left, right)
    ]
    normal = (speed_x, speed_y, speed_z)[direction]
    mass = (weight * density) * normal
    moment = [mass * speed_x, mass * speed_y, mass * speed_z]
    moment[direction] = moment[direction] + weight * pressure
    return [mass] + moment + [mass * enthalpy]


def kernel(
    n_gx,
    n_yz,
    state_in,
    register_in,
    out_register,
    out_filtered,
    state,
    register,
    prims,
    acc,
    xrecv,
    ysend,
    yrecv,
    sec,
    early,
    filt,
    srecv,
    ab,
    pab,
    chip,
    chips,
    inc,
    pinc,
    xs,
    xr,
    ys,
    yr,
    ss,
    sr,
    abs_,
    abr,
    cs,
    cr,
    ins,
    inr,
    local,
):
    nf, nx, ny, nz = state.shape
    n_ch = nz // LANES
    tiles = ny // ROWS
    zs = n_gx // 2
    me = lax.axis_index("gx")
    mine = lax.axis_index("yz")
    core = lax.rem(me, 2)
    chip_at = lax.div(me, 2)
    nxt = lax.rem(me + 1, n_gx)
    prv = lax.rem(me + n_gx - 1, n_gx)
    partner = me + 1 - 2 * core
    ynxt = lax.rem(mine + 1, n_yz)
    yprv = lax.rem(mine + n_yz - 1, n_yz)

    def chip_peer(d):
        return 2 * lax.rem(chip_at + (1 - 2 * core) * d + zs, zs) + core

    barrier = pltpu.get_barrier_semaphore()
    peers = [(prv, mine), (nxt, mine), (me, yprv), (me, ynxt)]
    peers += [(chip_peer(d), mine) for d in range(1, zs)]
    for peer in peers:
        pl.semaphore_signal(barrier, inc=1, device_id=peer, device_id_type=MESH)

    loads = [
        pltpu.make_async_copy(state_in.at[f], state.at[f], local.at[f]) for f in range(nf)
    ]
    loads += [
        pltpu.make_async_copy(register_in.at[f], register.at[f], local.at[nf + f])
        for f in range(nf)
    ]
    for load in loads:
        load.start()

    for f in range(nf):
        loads[f].wait()

        @pl.loop(0, nx, unroll=4)
        def _(x, f=f):
            for ch in range(n_ch):
                cols = pl.ds(ch * LANES, LANES)
                ysend[ch, 0, f, x] = state[f, x, pl.ds(0, ROWS), cols][:4]
                ysend[ch, 1, f, x] = state[f, x, pl.ds(ny - ROWS, ROWS), cols][4:]

    pl.semaphore_wait(barrier, len(peers))

    def remote(src, dst, send, recv, peer):
        return pltpu.make_async_remote_copy(
            src_ref=src,
            dst_ref=dst,
            send_sem=send,
            recv_sem=recv,
            device_id=peer,
            device_id_type=MESH,
        )

    def y_copies(ch):
        return [
            remote(
                ysend.at[ch, side],
                yrecv.at[ch, side],
                ys.at[ch, side],
                yr.at[ch, side],
                (me, (yprv, ynxt)[side]),
            )
            for side in range(2)
        ]

    ycopies = [y_copies(ch) for ch in range(n_ch)]
    xcopies = [
        remote(state.at[:, pl.ds(0, 4)], xrecv.at[0], xs.at[0], xr.at[0], (prv, mine)),
        remote(state.at[:, pl.ds(nx - 4, 4)], xrecv.at[1], xs.at[1], xr.at[1], (nxt, mine)),
    ]
    for copy in ycopies[0] + xcopies:
        copy.start()
    for ch in range(1, n_ch):
        for copy in ycopies[ch]:
            copy.start()

    weights = [-time_step * w for w in central_weights]

    @pl.loop(0, nx * tiles)
    def _(i):
        x = i // tiles
        rows = pl.ds(pl.multiple_of((i % tiles) * ROWS, ROWS), ROWS)
        own = primitives([state[f, x, rows, :] for f in range(nf)])
        for f in range(6):
            prims[f, x + 4, rows, :] = own[f]
        total = [jnp.zeros((ROWS, nz), jnp.float32) for _ in range(nf)]
        for l in range(1, 5):
            ahead = [pltpu.roll(q, nz - l, axis=1) for q in own]
            flux = pair_flux(own, ahead, 2, weights[l - 1])
            total = [t + (v - pltpu.roll(v, l, axis=1)) for t, v in zip(total, flux)]
        for f in range(nf):
            acc[f, x, rows, :] = total[f]

    place = lax.broadcasted_iota(jnp.int32, (ny, LANES), 0)

    @pl.loop(0, nx)
    def _(x):
        for ch in range(n_ch):
            cols = pl.ds(ch * LANES, LANES)
            own = [prims[f, x + 4, :, cols] for f in range(6)]
            total = [acc[f, x, :, cols] for f in range(nf)]
            for l in range(1, 5):
                ahead = [pltpu.roll(q, ny - l, axis=0) for q in own]
                inside = jnp.where(place < ny - l, weights[l - 1], 0.0)
                flux = pair_flux(own, ahead, 1, inside)
                total = [t + (v - pltpu.roll(v, l, axis=0)) for t, v in zip(total, flux)]
            for f in range(nf):
                acc[f, x, :, cols] = total[f]

    for copy in xcopies:
        copy.wait_recv()

    @pl.loop(0, 4 * tiles)
    def _(i):
        x = i // tiles
        rows = pl.ds(pl.multiple_of((i % tiles) * ROWS, ROWS), ROWS)
        for side in range(2):
            got = primitives([xrecv[side, f, x, rows, :] for f in range(nf)])
            for f in range(6):
                prims[f, x + (nx + 4, 0)[side], rows, :] = got[f]

    for load in loads[nf:]:
        load.wait()

    stencil, remainder, mu = filter_constants()
    rho = mu**nx
    low = lax.broadcasted_iota(jnp.int32, (ROWS, LANES), 0) < 4
    top, bottom = pl.ds(0, ROWS), pl.ds(ny - ROWS, ROWS)

    def inner(first, last):
        return jnp.where(low, last, first)

    def outer(first, last):
        return jnp.where(low, first, last)

    def x_pass(ch):
        cols = pl.ds(ch * LANES, LANES)

        @pl.loop(0, nx)
        def _(x):
            parts = []
            for rows in (top, bottom):
                own = [prims[f, x + 4, rows, cols] for f in range(6)]
                total = [acc[f, x, rows, cols] for f in range(nf)]
                for l in range(1, 5):
                    ahead = [prims[f, x + 4 + l, rows, cols] for f in range(6)]
                    behind = [prims[f, x + 4 - l, rows, cols] for f in range(6)]
                    up = pair_flux(own, ahead, 0, weights[l - 1])
                    down = pair_flux(behind, own, 0, weights[l - 1])
                    total = [t + (u - d) for t, u, d in zip(total, up, down)]
                parts.append(
                    [
                        register_decay * register[f, x, rows, cols] + total[f]
                        for f in range(nf)
                    ]
                )
            for f in range(nf):
                first, last = parts[0][f], parts[1][f]
                state_first, state_last = state[f, x, top, cols], state[f, x, bottom, cols]
                for piece, pick in ((ch, inner), (n_ch + ch, outer)):
                    value = pick(first, last)
                    early[piece, f, x] = value
                    sec[piece, f, x] = pick(state_first, state_last) + register_gain * value

    signs = []
    spot = lax.broadcasted_iota(jnp.int32, (ROWS, LANES), 0)
    for l in range(1, 5):
        w = weights[l - 1]
        signs.append(jnp.where(spot < l, -w, jnp.where(spot >= ROWS - l, w, 0.0)))

    def y_pass(ch):
        piece = n_ch + ch
        cols = pl.ds(ch * LANES, LANES)
        for copy in ycopies[ch]:
            copy.wait_recv()

        @pl.loop(0, nx, unroll=2)
        def _(x):
            halo = primitives(
                [
                    jnp.concatenate([yrecv[ch, 0, f, x], yrecv[ch, 1, f, x]], axis=0)
                    for f in range(nf)
                ]
            )
            own = [
                outer(prims[f, x + 4, top, cols], prims[f, x + 4, bottom, cols])
                for f in range(6)
            ]
            total = [jnp.zeros((ROWS, LANES), jnp.float32) for _ in range(nf)]
            for l in range(1, 5):
                across = [
                    jnp.where(low, pltpu.roll(q, l, axis=0), pltpu.roll(q, ROWS - l, axis=0))
                    if l < 4
                    else pltpu.roll(q, l, axis=0)
                    for q in halo
                ]
                flux = pair_flux(own, across, 1, signs[l - 1])
                total = [t + v for t, v in zip(total, flux)]
            for f in range(nf):
                new = early[piece, f, x] + total[f]
                sec[piece, f, x] = sec[piece, f, x] + register_gain * total[f]
                mid = early[ch, f, x]
                out_register[f, x, top, cols] = jnp.where(low, new, mid)
                out_register[f, x, bottom, cols] = jnp.where(low, mid, new)

    def section_copies(p):
        return [
            remote(
                sec.at[p, :, pl.ds(0, 2)],
                srecv.at[p, 0],
                ss.at[p, 0],
                sr.at[p, 0],
                (prv, mine),
            ),
            remote(
                sec.at[p, :, pl.ds(nx - 2, 2)],
                srecv.at[p, 1],
                ss.at[p, 1],
                sr.at[p, 1],
                (nxt, mine),
            ),
        ]

    def chip_copies(p):
        return [
            remote(
                chip.at[p],
                chips.at[p, d - 1],
                cs.at[p, d - 1],
                cr.at[p, d - 1],
                (chip_peer(d), mine),
            )
            for d in range(1, zs)
        ]

    pieces = range(2 * n_ch)
    scopies = [section_copies(p) for p in pieces]
    abcopies = [
        remote(ab.at[p], pab.at[p], abs_.at[p], abr.at[p], (partner, mine)) for p in pieces
    ]
    ccopies = [chip_copies(p) for p in pieces]
    icopies = [
        remote(inc.at[p, core], pinc.at[p], ins.at[p], inr.at[p], (partner, mine))
        for p in pieces
    ]

    def begin(p):
        for f in range(nf):
            ahead = sec[p, f, 0]
            back = sec[p, f, nx - 1]
            for j in range(1, nx):
                ahead = sec[p, f, j] + mu * ahead
                back = sec[p, f, nx - 1 - j] + mu * back
            ab[p, 0, f] = ahead
            ab[p, 1, f] = back
        abcopies[p].start()
        for copy in scopies[p]:
            copy.start()

    def across_chips(p):
        abcopies[p].wait_recv()
        for f in range(nf):
            chip[p, f] = pab[p, core, f] + rho * ab[p, core, f]
        for copy in ccopies[p]:
            copy.start()

    def incoming(p):
        for copy in ccopies[p]:
            copy.wait_recv()
        scale = 1.0 / (1.0 - rho ** (2 * zs))
        for f in range(nf):
            total = (scale * rho ** (2 * (zs - 1))) * chip[p, f]
            for d in range(1, zs):
                total = total + (scale * rho ** (2 * (d - 1))) * chips[p, d - 1, f]
            inc[p, core, f] = total
        icopies[p].start()

    def finish(p):
        for copy in scopies[p]:
            copy.wait()
        icopies[p].wait()
        for f in range(nf):
            inc[p, 1 - core, f] = pab[p, 1 - core, f] + rho * pinc[p, f]
        for f in range(nf):
            s = (
                [srecv[p, 1, f, 0], srecv[p, 1, f, 1]]
                + [sec[p, f, j] for j in range(nx)]
                + [srecv[p, 0, f, 0], srecv[p, 0, f, 1]]
            )
            left = inc[p, 0, f]
            for j in range(nx):
                left = s[j + 2] + mu * left
                near = (
                    stencil[0] * s[j + 2]
                    + stencil[1] * (s[j + 1] + s[j + 3])
                    + stencil[2] * (s[j] + s[j + 4])
                )
                filt[p, f, j] = near + remainder * left
            right = inc[p, 1, f]
            for j in reversed(range(nx)):
                value = filt[p, f, j] + (remainder * mu) * right
                if p < n_ch:
                    filt[p, f, j] = value
                else:
                    mid = filt[p - n_ch, f, j]
                    cols = pl.ds((p - n_ch) * LANES, LANES)
                    out_filtered[f, j, top, cols] = jnp.where(low, value, mid)
                    out_filtered[f, j, bottom, cols] = jnp.where(low, mid, value)
                right = s[j + 2] + mu * right

    chunks = range(n_ch)
    for ch in chunks:
        x_pass(ch)
        begin(ch)
    for ch in chunks:
        across_chips(ch)
    y_pass(0)
    begin(n_ch)
    for ch in chunks:
        incoming(ch)
    across_chips(n_ch)
    for ch in chunks:
        finish(ch)
    for ch in range(1, n_ch):
        y_pass(ch)
        begin(n_ch + ch)
        incoming(n_ch + ch - 1)
        across_chips(n_ch + ch)
        finish(n_ch + ch - 1)
    incoming(2 * n_ch - 1)
    finish(2 * n_ch - 1)

    for ch in chunks:
        for copy in ycopies[ch]:
            copy.wait_send()
    for p in pieces:
        abcopies[p].wait_send()
        for copy in ccopies[p]:
            copy.wait_send()
    for copy in xcopies:
        copy.wait_send()


def body(n_gx, n_yz, state, register):
    nf, nx, ny, nz = state.shape
    n_ch = nz // LANES
    n_p = 2 * n_ch
    zs = n_gx // 2
    f32 = jnp.float32
    dma = pltpu.SemaphoreType.DMA
    return pl.pallas_call(
        functools.partial(kernel, n_gx, n_yz),
        out_shape=[jax.ShapeDtypeStruct(state.shape, f32)] * 2,
        in_specs=[pl.BlockSpec(memory_space=pltpu.HBM)] * 2,
        out_specs=[pl.BlockSpec(memory_space=pltpu.VMEM)] * 2,
        scratch_shapes=[
            pltpu.VMEM((nf, nx, ny, nz), f32),
            pltpu.VMEM((nf, nx, ny, nz), f32),
            pltpu.VMEM((6, nx + 8, ny, nz), f32),
            pltpu.VMEM((nf, nx, ny, nz), f32),
            pltpu.VMEM((2, nf, 4, ny, nz), f32),
            pltpu.VMEM((n_ch, 2, nf, nx, 4, LANES), f32),
            pltpu.VMEM((n_ch, 2, nf, nx, 4, LANES), f32),
            pltpu.VMEM((n_p, nf, nx, ROWS, LANES), f32),
            pltpu.VMEM((n_p, nf, nx, ROWS, LANES), f32),
            pltpu.VMEM((n_p, nf, nx, ROWS, LANES), f32),
            pltpu.VMEM((n_p, 2, nf, 2, ROWS, LANES), f32),
            pltpu.VMEM((n_p, 2, nf, ROWS, LANES), f32),
            pltpu.VMEM((n_p, 2, nf, ROWS, LANES), f32),
            pltpu.VMEM((n_p, nf, ROWS, LANES), f32),
            pltpu.VMEM((n_p, zs - 1, nf, ROWS, LANES), f32),
            pltpu.VMEM((n_p, 2, nf, ROWS, LANES), f32),
            pltpu.VMEM((n_p, nf, ROWS, LANES), f32),
            dma((2,)),
            dma((2,)),
            dma((n_ch, 2)),
            dma((n_ch, 2)),
            dma((n_p, 2)),
            dma((n_p, 2)),
            dma((n_p,)),
            dma((n_p,)),
            dma((n_p, zs - 1)),
            dma((n_p, zs - 1)),
            dma((n_p,)),
            dma((n_p,)),
            dma((2 * nf,)),
        ],
        compiler_params=pltpu.CompilerParams(
            collective_id=0, has_side_effects=True, vmem_limit_bytes=40 * 1024 * 1024
        ),
    )(state, register)


def solution(mesh):
    spec = P(None, "gx", "yz", None)
    run = functools.partial(body, mesh.shape["gx"], mesh.shape["yz"])
    return jax.shard_map(
        lambda state, register: tuple(run(state, register)),
        mesh=mesh,
        in_specs=(spec, spec),
        out_specs=(spec, spec),
        check_vma=False,
    )
```

```python
import functools

import jax
import jax.numpy as jnp
from jax import lax
from jax.experimental import pallas as pl
from jax.experimental.pallas import tpu as pltpu
from jax.sharding import PartitionSpec as P

gamma_gas = 1.4
central_weights = (4.0 / 5.0, -1.0 / 5.0, 4.0 / 105.0, -1.0 / 280.0)
filter_alpha = 0.49
register_decay = -5.0 / 9.0
register_gain = 15.0 / 16.0
time_step = 0.2
MESH = pl.DeviceIdType.MESH
LANES = 128
ROWS = 8
n_products = 18
vmem_limit = 56 * 1024 * 1024


def filter_constants():
    alpha = filter_alpha
    a0 = (11.0 + 10.0 * alpha) / 16.0
    a1 = (15.0 + 34.0 * alpha) / 32.0
    a2 = (-3.0 + 6.0 * alpha) / 16.0
    a3 = (1.0 - 2.0 * alpha) / 32.0
    q2 = 4.0 * a3 / (2.0 * alpha)
    q1 = (2.0 * a2 - q2) / (2.0 * alpha)
    q0 = (a1 - 3.0 * a3 - q1) / (2.0 * alpha)
    rest = a0 - a2 - q0
    mu = (-1.0 + (1.0 - 4.0 * alpha * alpha) ** 0.5) / (2.0 * alpha)
    kappa = (1.0 + mu * mu) / (1.0 - mu * mu)
    return (q0 + 0.5 * q2, 0.5 * q1, 0.25 * q2), kappa * rest, mu


def split_products(fields):
    density, mom_x, mom_y, mom_z, energy = fields
    inverse = 1.0 / density
    u, v, w = mom_x * inverse, mom_y * inverse, mom_z * inverse
    pressure = (gamma_gas - 1.0) * (energy - 0.5 * (mom_x * u + mom_y * v + mom_z * w))
    total = energy + pressure
    h = total * inverse
    prims = [density, 0.5 * u, 0.5 * v, 0.5 * w, pressure, 0.5 * h]
    return prims, [
        density, w, mom_z,
        mom_z * u, w * u, mom_x, u,
        mom_z * v, w * v, mom_y, v,
        mom_z * w, w * w,
        mom_z * h, w * h, total, h,
        pressure,
    ]


def split_residual(prims, d, scale):
    density, u, v, w, _, h = prims
    u, v, w, h = u + u, v + v, w + w, h + h
    mom = density * w
    mass = d[2] + density * d[1] + w * d[0]

    def moment(q, d_mq, d_wq, d_rq, d_q):
        return scale * (d_mq + density * d_wq + w * d_rq + q * mass + mom * d_q)

    return [
        (2.0 * scale) * mass,
        moment(u, d[3], d[4], d[5], d[6]),
        moment(v, d[7], d[8], d[9], d[10]),
        moment(w, d[11], d[12], d[2], d[1]) + (4.0 * scale) * d[17],
        moment(h, d[13], d[14], d[15], d[16]),
    ]


def primitives(fields):
    density = fields[0]
    inverse = 1.0 / density
    speeds = [fields[i] * inverse for i in (1, 2, 3)]
    kinetic = 0.5 * (
        fields[1] * speeds[0] + fields[2] * speeds[1] + fields[3] * speeds[2]
    )
    pressure = (gamma_gas - 1.0) * (fields[4] - kinetic)
    enthalpy = (fields[4] + pressure) * (0.5 * inverse)
    return [density] + [0.5 * speed for speed in speeds] + [pressure, enthalpy]


def pair_flux(left, right, direction, weight):
    density, speed_x, speed_y, speed_z, pressure, enthalpy = [
        one + other for one, other in zip(left, right)
    ]
    normal = (speed_x, speed_y, speed_z)[direction]
    mass = (weight * density) * normal
    moment = [mass * speed_x, mass * speed_y, mass * speed_z]
    moment[direction] = moment[direction] + weight * pressure
    return [mass] + moment + [mass * enthalpy]


def kernel(
    n_gx,
    n_yz,
    state_in,
    register_in,
    out_register,
    out_filtered,
    state,
    register,
    prims,
    acc,
    xrecv,
    ysend,
    yrecv,
    sec,
    early,
    filt,
    srecv,
    ab,
    pab,
    chip,
    chips,
    inc,
    pinc,
    xs,
    xr,
    ys,
    yr,
    ss,
    sr,
    abs_,
    abr,
    cs,
    cr,
    ins,
    inr,
    local,
    matrix,
    high,
    rest,
    deriv,
    reg_out,
    filt_out,
):
    nf, nx, ny, nz = state.shape
    n_ch = nz // LANES
    tiles = ny // ROWS
    zs = n_gx // 2
    me = lax.axis_index("gx")
    mine = lax.axis_index("yz")
    core = lax.rem(me, 2)
    chip_at = lax.div(me, 2)
    nxt = lax.rem(me + 1, n_gx)
    prv = lax.rem(me + n_gx - 1, n_gx)
    partner = me + 1 - 2 * core
    ynxt = lax.rem(mine + 1, n_yz)
    yprv = lax.rem(mine + n_yz - 1, n_yz)

    def chip_peer(d):
        return 2 * lax.rem(chip_at + (1 - 2 * core) * d + zs, zs) + core

    barrier = pltpu.get_barrier_semaphore()
    peers = [(prv, mine), (nxt, mine), (me, yprv), (me, ynxt)]
    peers += [(chip_peer(d), mine) for d in range(1, zs)]
    for peer in peers:
        pl.semaphore_signal(barrier, inc=1, device_id=peer, device_id_type=MESH)

    loads = [
        pltpu.make_async_copy(state_in.at[f], state.at[f], local.at[f]) for f in range(nf)
    ]
    loads += [
        pltpu.make_async_copy(register_in.at[f], register.at[f], local.at[nf + f])
        for f in range(nf)
    ]
    for load in loads:
        load.start()

    gap = lax.broadcasted_iota(jnp.int32, (nz, nz), 0) - lax.broadcasted_iota(
        jnp.int32, (nz, nz), 1
    )
    gap = jnp.where(gap < 0, gap + nz, gap)
    entries = jnp.zeros((nz, nz), jnp.float32)
    for l in range(1, 5):
        whole = float(round(840.0 * central_weights[l - 1]))
        entries = jnp.where(gap == l, whole, jnp.where(gap == nz - l, -whole, entries))
    matrix[...] = entries.astype(jnp.bfloat16)

    for f in range(nf):
        loads[f].wait()

        @pl.loop(0, nx, unroll=4)
        def _(x, f=f):
            for ch in range(n_ch):
                cols = pl.ds(ch * LANES, LANES)
                ysend[ch, 0, f, x] = state[f, x, pl.ds(0, ROWS), cols][:4]
                ysend[ch, 1, f, x] = state[f, x, pl.ds(ny - ROWS, ROWS), cols][4:]

    pl.semaphore_wait(barrier, len(peers))

    def remote(src, dst, send, recv, peer):
        return pltpu.make_async_remote_copy(
            src_ref=src,
            dst_ref=dst,
            send_sem=send,
            recv_sem=recv,
            device_id=peer,
            device_id_type=MESH,
        )

    def y_copies(ch):
        return [
            remote(
                ysend.at[ch, side],
                yrecv.at[ch, side],
                ys.at[ch, side],
                yr.at[ch, side],
                (me, (yprv, ynxt)[side]),
            )
            for side in range(2)
        ]

    ycopies = [y_copies(ch) for ch in range(n_ch)]
    xcopies = [
        remote(state.at[:, pl.ds(0, 4)], xrecv.at[0], xs.at[0], xr.at[0], (prv, mine)),
        remote(state.at[:, pl.ds(nx - 4, 4)], xrecv.at[1], xs.at[1], xr.at[1], (nxt, mine)),
    ]
    for copy in ycopies[0] + xcopies:
        copy.start()
    for ch in range(1, n_ch):
        for copy in ycopies[ch]:
            copy.start()

    weights = [-time_step * w for w in central_weights]

    @pl.loop(0, nx)
    def _(x):
        rows = pl.ds(pl.multiple_of(x * ny, ny), ny)
        own, products = split_products([state[f, x] for f in range(nf)])
        for f in range(6):
            prims[f, x + 4] = own[f]
        for k, value in enumerate(products):
            part = value.astype(jnp.bfloat16)
            high[k, rows, :] = part
            rest[k, rows, :] = (value - part.astype(jnp.float32)).astype(jnp.bfloat16)

    @pl.loop(0, n_products)
    def _(k):
        whole = jnp.dot(high[k], matrix[...], preferred_element_type=jnp.float32)
        deriv[k] = whole + jnp.dot(rest[k], matrix[...], preferred_element_type=jnp.float32)

    @pl.loop(0, nx * tiles)
    def _(i):
        x = i // tiles
        rows = pl.ds(pl.multiple_of((i % tiles) * ROWS, ROWS), ROWS)
        flat = pl.ds(pl.multiple_of(i * ROWS, ROWS), ROWS)
        total = split_residual(
            [prims[f, x + 4, rows, :] for f in range(6)],
            [deriv[k, flat, :] for k in range(n_products)],
            -time_step / (4.0 * 840.0),
        )
        for f in range(nf):
            acc[f, x, rows, :] = total[f]

    place = lax.broadcasted_iota(jnp.int32, (ny, LANES), 0)

    @pl.loop(0, nx)
    def _(x):
        for ch in range(n_ch):
            cols = pl.ds(ch * LANES, LANES)
            own = [prims[f, x + 4, :, cols] for f in range(6)]
            total = [acc[f, x, :, cols] for f in range(nf)]
            for l in range(1, 5):
                ahead = [pltpu.roll(q, ny - l, axis=0) for q in own]
                inside = jnp.where(place < ny - l, weights[l - 1], 0.0)
                flux = pair_flux(own, ahead, 1, inside)
                total = [t + (v - pltpu.roll(v, l, axis=0)) for t, v in zip(total, flux)]
            for f in range(nf):
                acc[f, x, :, cols] = total[f]

    for copy in xcopies:
        copy.wait_recv()

    @pl.loop(0, 4 * tiles)
    def _(i):
        x = i // tiles
        rows = pl.ds(pl.multiple_of((i % tiles) * ROWS, ROWS), ROWS)
        for side in range(2):
            got = primitives([xrecv[side, f, x, rows, :] for f in range(nf)])
            for f in range(6):
                prims[f, x + (nx + 4, 0)[side], rows, :] = got[f]

    for load in loads[nf:]:
        load.wait()

    stencil, remainder, mu = filter_constants()
    rho = mu**nx
    low = lax.broadcasted_iota(jnp.int32, (ROWS, LANES), 0) < 4
    top, bottom = pl.ds(0, ROWS), pl.ds(ny - ROWS, ROWS)

    def inner(first, last):
        return jnp.where(low, last, first)

    def outer(first, last):
        return jnp.where(low, first, last)

    def x_pass(ch):
        cols = pl.ds(ch * LANES, LANES)

        @pl.loop(0, nx)
        def _(x):
            parts = []
            for rows in (top, bottom):
                own = [prims[f, x + 4, rows, cols] for f in range(6)]
                total = [acc[f, x, rows, cols] for f in range(nf)]
                for l in range(1, 5):
                    ahead = [prims[f, x + 4 + l, rows, cols] for f in range(6)]
                    behind = [prims[f, x + 4 - l, rows, cols] for f in range(6)]
                    up = pair_flux(own, ahead, 0, weights[l - 1])
                    down = pair_flux(behind, own, 0, weights[l - 1])
                    total = [t + (u - d) for t, u, d in zip(total, up, down)]
                parts.append(
                    [
                        register_decay * register[f, x, rows, cols] + total[f]
                        for f in range(nf)
                    ]
                )
            for f in range(nf):
                first, last = parts[0][f], parts[1][f]
                state_first, state_last = state[f, x, top, cols], state[f, x, bottom, cols]
                for piece, pick in ((ch, inner), (n_ch + ch, outer)):
                    value = pick(first, last)
                    early[piece, f, x] = value
                    sec[piece, f, x] = pick(state_first, state_last) + register_gain * value

    signs = []
    spot = lax.broadcasted_iota(jnp.int32, (ROWS, LANES), 0)
    for l in range(1, 5):
        w = weights[l - 1]
        signs.append(jnp.where(spot < l, -w, jnp.where(spot >= ROWS - l, w, 0.0)))

    def y_pass(ch):
        piece = n_ch + ch
        cols = pl.ds(ch * LANES, LANES)
        for copy in ycopies[ch]:
            copy.wait_recv()

        @pl.loop(0, nx, unroll=2)
        def _(x):
            halo = primitives(
                [
                    jnp.concatenate([yrecv[ch, 0, f, x], yrecv[ch, 1, f, x]], axis=0)
                    for f in range(nf)
                ]
            )
            own = [
                outer(prims[f, x + 4, top, cols], prims[f, x + 4, bottom, cols])
                for f in range(6)
            ]
            total = [jnp.zeros((ROWS, LANES), jnp.float32) for _ in range(nf)]
            for l in range(1, 5):
                across = [
                    jnp.where(low, pltpu.roll(q, l, axis=0), pltpu.roll(q, ROWS - l, axis=0))
                    if l < 4
                    else pltpu.roll(q, l, axis=0)
                    for q in halo
                ]
                flux = pair_flux(own, across, 1, signs[l - 1])
                total = [t + v for t, v in zip(total, flux)]
            for f in range(nf):
                new = early[piece, f, x] + total[f]
                sec[piece, f, x] = sec[piece, f, x] + register_gain * total[f]
                mid = early[ch, f, x]
                reg_out[f, x, top, cols] = jnp.where(low, new, mid)
                reg_out[f, x, bottom, cols] = jnp.where(low, mid, new)

    def section_copies(p):
        return [
            remote(
                sec.at[p, :, pl.ds(0, 2)],
                srecv.at[p, 0],
                ss.at[p, 0],
                sr.at[p, 0],
                (prv, mine),
            ),
            remote(
                sec.at[p, :, pl.ds(nx - 2, 2)],
                srecv.at[p, 1],
                ss.at[p, 1],
                sr.at[p, 1],
                (nxt, mine),
            ),
        ]

    def chip_copies(p):
        return [
            remote(
                chip.at[p],
                chips.at[p, d - 1],
                cs.at[p, d - 1],
                cr.at[p, d - 1],
                (chip_peer(d), mine),
            )
            for d in range(1, zs)
        ]

    pieces = range(2 * n_ch)
    scopies = [section_copies(p) for p in pieces]
    abcopies = [
        remote(ab.at[p], pab.at[p], abs_.at[p], abr.at[p], (partner, mine)) for p in pieces
    ]
    ccopies = [chip_copies(p) for p in pieces]
    icopies = [
        remote(inc.at[p, core], pinc.at[p], ins.at[p], inr.at[p], (partner, mine))
        for p in pieces
    ]

    def begin(p):
        for f in range(nf):
            ahead = sec[p, f, 0]
            back = sec[p, f, nx - 1]
            for j in range(1, nx):
                ahead = sec[p, f, j] + mu * ahead
                back = sec[p, f, nx - 1 - j] + mu * back
            ab[p, 0, f] = ahead
            ab[p, 1, f] = back
        abcopies[p].start()
        for copy in scopies[p]:
            copy.start()

    def across_chips(p):
        abcopies[p].wait_recv()
        for f in range(nf):
            chip[p, f] = pab[p, core, f] + rho * ab[p, core, f]
        for copy in ccopies[p]:
            copy.start()

    def incoming(p):
        for copy in ccopies[p]:
            copy.wait_recv()
        scale = 1.0 / (1.0 - rho ** (2 * zs))
        for f in range(nf):
            total = (scale * rho ** (2 * (zs - 1))) * chip[p, f]
            for d in range(1, zs):
                total = total + (scale * rho ** (2 * (d - 1))) * chips[p, d - 1, f]
            inc[p, core, f] = total
        icopies[p].start()

    def finish(p):
        for copy in scopies[p]:
            copy.wait()
        icopies[p].wait()
        for f in range(nf):
            inc[p, 1 - core, f] = pab[p, 1 - core, f] + rho * pinc[p, f]
        for f in range(nf):
            s = (
                [srecv[p, 1, f, 0], srecv[p, 1, f, 1]]
                + [sec[p, f, j] for j in range(nx)]
                + [srecv[p, 0, f, 0], srecv[p, 0, f, 1]]
            )
            left = inc[p, 0, f]
            for j in range(nx):
                left = s[j + 2] + mu * left
                near = (
                    stencil[0] * s[j + 2]
                    + stencil[1] * (s[j + 1] + s[j + 3])
                    + stencil[2] * (s[j] + s[j + 4])
                )
                filt[p, f, j] = near + remainder * left
            right = inc[p, 1, f]
            for j in reversed(range(nx)):
                value = filt[p, f, j] + (remainder * mu) * right
                if p < n_ch:
                    filt[p, f, j] = value
                else:
                    mid = filt[p - n_ch, f, j]
                    cols = pl.ds((p - n_ch) * LANES, LANES)
                    filt_out[f, j, top, cols] = jnp.where(low, value, mid)
                    filt_out[f, j, bottom, cols] = jnp.where(low, mid, value)
                right = s[j + 2] + mu * right

    chunks = range(n_ch)

    def result_copy(src, dst, ch, sem):
        cols = pl.ds(ch * LANES, LANES)
        return pltpu.make_async_copy(
            src.at[:, :, :, cols], dst.at[:, :, :, cols], local.at[sem]
        )

    reg_copies = [result_copy(reg_out, out_register, ch, 2 * nf + ch) for ch in chunks]
    filt_copies = [
        result_copy(filt_out, out_filtered, ch, 2 * nf + n_ch + ch) for ch in chunks
    ]

    for ch in chunks:
        x_pass(ch)
        begin(ch)
    for ch in chunks:
        across_chips(ch)
    y_pass(0)
    begin(n_ch)
    reg_copies[0].start()
    for ch in chunks:
        incoming(ch)
    across_chips(n_ch)
    for ch in chunks:
        finish(ch)
    for ch in range(1, n_ch):
        y_pass(ch)
        begin(n_ch + ch)
        reg_copies[ch].start()
        incoming(n_ch + ch - 1)
        across_chips(n_ch + ch)
        finish(n_ch + ch - 1)
        filt_copies[ch - 1].start()
    incoming(2 * n_ch - 1)
    finish(2 * n_ch - 1)
    filt_copies[n_ch - 1].start()

    for ch in chunks:
        for copy in ycopies[ch]:
            copy.wait_send()
    for p in pieces:
        abcopies[p].wait_send()
        for copy in ccopies[p]:
            copy.wait_send()
    for copy in xcopies:
        copy.wait_send()
    for copy in reg_copies + filt_copies:
        copy.wait()


def hand_out(first, second, out_first, out_second, sems):
    copies = []
    for f in range(first.shape[0]):
        for k, (src, dst) in enumerate(((first, out_first), (second, out_second))):
            copies.append(pltpu.make_async_copy(src.at[f], dst.at[f], sems.at[k, f]))
    for copy in copies:
        copy.start()
    for copy in copies:
        copy.wait()


def body(n_gx, n_yz, state, register):
    nf, nx, ny, nz = state.shape
    n_ch = nz // LANES
    n_p = 2 * n_ch
    zs = n_gx // 2
    f32 = jnp.float32
    dma = pltpu.SemaphoreType.DMA
    results = pl.pallas_call(
        functools.partial(kernel, n_gx, n_yz),
        out_shape=[jax.ShapeDtypeStruct(state.shape, f32)] * 2,
        in_specs=[pl.BlockSpec(memory_space=pl.ANY)] * 2,
        out_specs=[pl.BlockSpec(memory_space=pl.ANY)] * 2,
        scratch_shapes=[
            pltpu.VMEM((nf, nx, ny, nz), f32),
            pltpu.VMEM((nf, nx, ny, nz), f32),
            pltpu.VMEM((6, nx + 8, ny, nz), f32),
            pltpu.VMEM((nf, nx, ny, nz), f32),
            pltpu.VMEM((2, nf, 4, ny, nz), f32),
            pltpu.VMEM((n_ch, 2, nf, nx, 4, LANES), f32),
            pltpu.VMEM((n_ch, 2, nf, nx, 4, LANES), f32),
            pltpu.VMEM((n_p, nf, nx, ROWS, LANES), f32),
            pltpu.VMEM((n_p, nf, nx, ROWS, LANES), f32),
            pltpu.VMEM((n_p, nf, nx, ROWS, LANES), f32),
            pltpu.VMEM((n_p, 2, nf, 2, ROWS, LANES), f32),
            pltpu.VMEM((n_p, 2, nf, ROWS, LANES), f32),
            pltpu.VMEM((n_p, 2, nf, ROWS, LANES), f32),
            pltpu.VMEM((n_p, nf, ROWS, LANES), f32),
            pltpu.VMEM((n_p, zs - 1, nf, ROWS, LANES), f32),
            pltpu.VMEM((n_p, 2, nf, ROWS, LANES), f32),
            pltpu.VMEM((n_p, nf, ROWS, LANES), f32),
            dma((2,)),
            dma((2,)),
            dma((n_ch, 2)),
            dma((n_ch, 2)),
            dma((n_p, 2)),
            dma((n_p, 2)),
            dma((n_p,)),
            dma((n_p,)),
            dma((n_p, zs - 1)),
            dma((n_p, zs - 1)),
            dma((n_p,)),
            dma((n_p,)),
            dma((2 * nf + 2 * n_ch,)),
            pltpu.VMEM((nz, nz), jnp.bfloat16),
            pltpu.VMEM((n_products, nx * ny, nz), jnp.bfloat16),
            pltpu.VMEM((n_products, nx * ny, nz), jnp.bfloat16),
            pltpu.VMEM((n_products, nx * ny, nz), f32),
            pltpu.VMEM((nf, nx, ny, nz), f32),
            pltpu.VMEM((nf, nx, ny, nz), f32),
        ],
        compiler_params=pltpu.CompilerParams(
            collective_id=0, has_side_effects=True, vmem_limit_bytes=vmem_limit
        ),
    )(state, register)
    return pl.pallas_call(
        hand_out,
        out_shape=[jax.ShapeDtypeStruct(state.shape, f32)] * 2,
        in_specs=[pl.BlockSpec(memory_space=pl.ANY)] * 2,
        out_specs=[pl.BlockSpec(memory_space=pl.ANY)] * 2,
        scratch_shapes=[dma((2, nf))],
        compiler_params=pltpu.CompilerParams(vmem_limit_bytes=vmem_limit),
    )(*results)


def solution(mesh):
    spec = P(None, "gx", "yz", None)
    run = functools.partial(body, mesh.shape["gx"], mesh.shape["yz"])
    return jax.shard_map(
        lambda state, register: tuple(run(state, register)),
        mesh=mesh,
        in_specs=(spec, spec),
        out_specs=(spec, spec),
        check_vma=False,
    )
```

```python
import functools

import jax
import jax.numpy as jnp
from jax import lax
from jax.experimental import pallas as pl
from jax.experimental.pallas import tpu as pltpu
from jax.sharding import PartitionSpec as P

gamma_gas = 1.4
central_weights = (4.0 / 5.0, -1.0 / 5.0, 4.0 / 105.0, -1.0 / 280.0)
filter_alpha = 0.49
register_decay = -5.0 / 9.0
register_gain = 15.0 / 16.0
time_step = 0.2
MESH = pl.DeviceIdType.MESH
LANES = 128
ROWS = 8
n_products = 18
vmem_limit = 51 * 1024 * 1024


def filter_constants():
    alpha = filter_alpha
    a0 = (11.0 + 10.0 * alpha) / 16.0
    a1 = (15.0 + 34.0 * alpha) / 32.0
    a2 = (-3.0 + 6.0 * alpha) / 16.0
    a3 = (1.0 - 2.0 * alpha) / 32.0
    q2 = 4.0 * a3 / (2.0 * alpha)
    q1 = (2.0 * a2 - q2) / (2.0 * alpha)
    q0 = (a1 - 3.0 * a3 - q1) / (2.0 * alpha)
    rest = a0 - a2 - q0
    mu = (-1.0 + (1.0 - 4.0 * alpha * alpha) ** 0.5) / (2.0 * alpha)
    kappa = (1.0 + mu * mu) / (1.0 - mu * mu)
    return (q0 + 0.5 * q2, 0.5 * q1, 0.25 * q2), kappa * rest, mu


def split_products(fields):
    density, mom_x, mom_y, mom_z, energy = fields
    inverse = 1.0 / density
    u, v, w = mom_x * inverse, mom_y * inverse, mom_z * inverse
    pressure = (gamma_gas - 1.0) * (energy - 0.5 * (mom_x * u + mom_y * v + mom_z * w))
    total = energy + pressure
    h = total * inverse
    prims = [density, 0.5 * u, 0.5 * v, 0.5 * w, pressure, 0.5 * h]
    return prims, [
        density, w, mom_z,
        mom_z * u, w * u, mom_x, u,
        mom_z * v, w * v, mom_y, v,
        mom_z * w, w * w,
        mom_z * h, w * h, total, h,
        pressure,
    ]


def split_residual(prims, d, scale):
    density, u, v, w, _, h = prims
    u, v, w, h = u + u, v + v, w + w, h + h
    mom = density * w
    mass = d[2] + density * d[1] + w * d[0]

    def moment(q, d_mq, d_wq, d_rq, d_q):
        return scale * (d_mq + density * d_wq + w * d_rq + q * mass + mom * d_q)

    return [
        (2.0 * scale) * mass,
        moment(u, d[3], d[4], d[5], d[6]),
        moment(v, d[7], d[8], d[9], d[10]),
        moment(w, d[11], d[12], d[2], d[1]) + (4.0 * scale) * d[17],
        moment(h, d[13], d[14], d[15], d[16]),
    ]


def primitives(fields):
    density = fields[0]
    inverse = 1.0 / density
    speeds = [fields[i] * inverse for i in (1, 2, 3)]
    kinetic = 0.5 * (
        fields[1] * speeds[0] + fields[2] * speeds[1] + fields[3] * speeds[2]
    )
    pressure = (gamma_gas - 1.0) * (fields[4] - kinetic)
    enthalpy = (fields[4] + pressure) * (0.5 * inverse)
    return [density] + [0.5 * speed for speed in speeds] + [pressure, enthalpy]


def pair_flux(left, right, direction, weight):
    density, speed_x, speed_y, speed_z, pressure, enthalpy = [
        one + other for one, other in zip(left, right)
    ]
    normal = (speed_x, speed_y, speed_z)[direction]
    mass = (weight * density) * normal
    moment = [mass * speed_x, mass * speed_y, mass * speed_z]
    moment[direction] = moment[direction] + weight * pressure
    return [mass] + moment + [mass * enthalpy]


def kernel(
    n_gx,
    n_yz,
    state_in,
    register_in,
    reg_out,
    filt_out,
    state,
    register,
    prims,
    acc,
    xrecv,
    ysend,
    yrecv,
    sec,
    early,
    filt,
    srecv,
    ab,
    pab,
    chip,
    chips,
    inc,
    pinc,
    xs,
    xr,
    ys,
    yr,
    ss,
    sr,
    abs_,
    abr,
    cs,
    cr,
    ins,
    inr,
    local,
    matrix,
    high,
    rest,
    deriv,
):
    nf, nx, ny, nz = state.shape
    n_ch = nz // LANES
    tiles = ny // ROWS
    zs = n_gx // 2
    me = lax.axis_index("gx")
    mine = lax.axis_index("yz")
    core = lax.rem(me, 2)
    chip_at = lax.div(me, 2)
    nxt = lax.rem(me + 1, n_gx)
    prv = lax.rem(me + n_gx - 1, n_gx)
    partner = me + 1 - 2 * core
    ynxt = lax.rem(mine + 1, n_yz)
    yprv = lax.rem(mine + n_yz - 1, n_yz)

    def chip_peer(d):
        return 2 * lax.rem(chip_at + (1 - 2 * core) * d + zs, zs) + core

    barrier = pltpu.get_barrier_semaphore()
    peers = [(prv, mine), (nxt, mine), (me, yprv), (me, ynxt)]
    peers += [(chip_peer(d), mine) for d in range(1, zs)]
    for peer in peers:
        pl.semaphore_signal(barrier, inc=1, device_id=peer, device_id_type=MESH)

    loads = [
        pltpu.make_async_copy(state_in.at[f], state.at[f], local.at[f]) for f in range(nf)
    ]
    loads += [
        pltpu.make_async_copy(register_in.at[f], register.at[f], local.at[nf + f])
        for f in range(nf)
    ]
    for load in loads:
        load.start()

    gap = lax.broadcasted_iota(jnp.int32, (nz, nz), 0) - lax.broadcasted_iota(
        jnp.int32, (nz, nz), 1
    )
    gap = jnp.where(gap < 0, gap + nz, gap)
    entries = jnp.zeros((nz, nz), jnp.float32)
    for l in range(1, 5):
        whole = float(round(840.0 * central_weights[l - 1]))
        entries = jnp.where(gap == l, whole, jnp.where(gap == nz - l, -whole, entries))
    matrix[...] = entries.astype(jnp.bfloat16)

    for f in range(nf):
        loads[f].wait()

        @pl.loop(0, nx, unroll=4)
        def _(x, f=f):
            for ch in range(n_ch):
                cols = pl.ds(ch * LANES, LANES)
                ysend[ch, 0, f, x] = state[f, x, pl.ds(0, ROWS), cols][:4]
                ysend[ch, 1, f, x] = state[f, x, pl.ds(ny - ROWS, ROWS), cols][4:]

    pl.semaphore_wait(barrier, len(peers))

    def remote(src, dst, send, recv, peer):
        return pltpu.make_async_remote_copy(
            src_ref=src,
            dst_ref=dst,
            send_sem=send,
            recv_sem=recv,
            device_id=peer,
            device_id_type=MESH,
        )

    def y_copies(ch):
        return [
            remote(
                ysend.at[ch, side],
                yrecv.at[ch, side],
                ys.at[ch, side],
                yr.at[ch, side],
                (me, (yprv, ynxt)[side]),
            )
            for side in range(2)
        ]

    ycopies = [y_copies(ch) for ch in range(n_ch)]
    xcopies = [
        remote(state.at[:, pl.ds(0, 4)], xrecv.at[0], xs.at[0], xr.at[0], (prv, mine)),
        remote(state.at[:, pl.ds(nx - 4, 4)], xrecv.at[1], xs.at[1], xr.at[1], (nxt, mine)),
    ]
    for copy in ycopies[0] + xcopies:
        copy.start()
    for ch in range(1, n_ch):
        for copy in ycopies[ch]:
            copy.start()

    weights = [-time_step * w for w in central_weights]

    @pl.loop(0, nx)
    def _(x):
        rows = pl.ds(pl.multiple_of(x * ny, ny), ny)
        own, products = split_products([state[f, x] for f in range(nf)])
        for f in range(6):
            prims[f, x + 4] = own[f]
        for k, value in enumerate(products):
            part = value.astype(jnp.bfloat16)
            high[k, rows, :] = part
            rest[k, rows, :] = (value - part.astype(jnp.float32)).astype(jnp.bfloat16)

    @pl.loop(0, n_products)
    def _(k):
        whole = jnp.dot(high[k], matrix[...], preferred_element_type=jnp.float32)
        deriv[k] = whole + jnp.dot(rest[k], matrix[...], preferred_element_type=jnp.float32)

    @pl.loop(0, nx * tiles)
    def _(i):
        x = i // tiles
        rows = pl.ds(pl.multiple_of((i % tiles) * ROWS, ROWS), ROWS)
        flat = pl.ds(pl.multiple_of(i * ROWS, ROWS), ROWS)
        total = split_residual(
            [prims[f, x + 4, rows, :] for f in range(6)],
            [deriv[k, flat, :] for k in range(n_products)],
            -time_step / (4.0 * 840.0),
        )
        for f in range(nf):
            acc[f, x, rows, :] = total[f]

    place = lax.broadcasted_iota(jnp.int32, (ny, LANES), 0)

    @pl.loop(0, nx)
    def _(x):
        for ch in range(n_ch):
            cols = pl.ds(ch * LANES, LANES)
            own = [prims[f, x + 4, :, cols] for f in range(6)]
            total = [acc[f, x, :, cols] for f in range(nf)]
            for l in range(1, 5):
                ahead = [pltpu.roll(q, ny - l, axis=0) for q in own]
                inside = jnp.where(place < ny - l, weights[l - 1], 0.0)
                flux = pair_flux(own, ahead, 1, inside)
                total = [t + (v - pltpu.roll(v, l, axis=0)) for t, v in zip(total, flux)]
            for f in range(nf):
                acc[f, x, :, cols] = total[f]

    for copy in xcopies:
        copy.wait_recv()

    @pl.loop(0, 4 * tiles)
    def _(i):
        x = i // tiles
        rows = pl.ds(pl.multiple_of((i % tiles) * ROWS, ROWS), ROWS)
        for side in range(2):
            got = primitives([xrecv[side, f, x, rows, :] for f in range(nf)])
            for f in range(6):
                prims[f, x + (nx + 4, 0)[side], rows, :] = got[f]

    for load in loads[nf:]:
        load.wait()

    stencil, remainder, mu = filter_constants()
    rho = mu**nx
    low = lax.broadcasted_iota(jnp.int32, (ROWS, LANES), 0) < 4
    top, bottom = pl.ds(0, ROWS), pl.ds(ny - ROWS, ROWS)

    def inner(first, last):
        return jnp.where(low, last, first)

    def outer(first, last):
        return jnp.where(low, first, last)

    def x_pass(ch):
        cols = pl.ds(ch * LANES, LANES)

        @pl.loop(0, nx)
        def _(x):
            parts = []
            for rows in (top, bottom):
                own = [prims[f, x + 4, rows, cols] for f in range(6)]
                total = [acc[f, x, rows, cols] for f in range(nf)]
                for l in range(1, 5):
                    ahead = [prims[f, x + 4 + l, rows, cols] for f in range(6)]
                    behind = [prims[f, x + 4 - l, rows, cols] for f in range(6)]
                    up = pair_flux(own, ahead, 0, weights[l - 1])
                    down = pair_flux(behind, own, 0, weights[l - 1])
                    total = [t + (u - d) for t, u, d in zip(total, up, down)]
                parts.append(
                    [
                        register_decay * register[f, x, rows, cols] + total[f]
                        for f in range(nf)
                    ]
                )
            for f in range(nf):
                first, last = parts[0][f], parts[1][f]
                state_first, state_last = state[f, x, top, cols], state[f, x, bottom, cols]
                for piece, pick in ((ch, inner), (n_ch + ch, outer)):
                    value = pick(first, last)
                    early[piece, f, x] = value
                    sec[piece, f, x] = pick(state_first, state_last) + register_gain * value

    signs = []
    spot = lax.broadcasted_iota(jnp.int32, (ROWS, LANES), 0)
    for l in range(1, 5):
        w = weights[l - 1]
        signs.append(jnp.where(spot < l, -w, jnp.where(spot >= ROWS - l, w, 0.0)))

    def y_pass(ch):
        piece = n_ch + ch
        cols = pl.ds(ch * LANES, LANES)
        for copy in ycopies[ch]:
            copy.wait_recv()

        @pl.loop(0, nx, unroll=2)
        def _(x):
            halo = primitives(
                [
                    jnp.concatenate([yrecv[ch, 0, f, x], yrecv[ch, 1, f, x]], axis=0)
                    for f in range(nf)
                ]
            )
            own = [
                outer(prims[f, x + 4, top, cols], prims[f, x + 4, bottom, cols])
                for f in range(6)
            ]
            total = [jnp.zeros((ROWS, LANES), jnp.float32) for _ in range(nf)]
            for l in range(1, 5):
                across = [
                    jnp.where(low, pltpu.roll(q, l, axis=0), pltpu.roll(q, ROWS - l, axis=0))
                    if l < 4
                    else pltpu.roll(q, l, axis=0)
                    for q in halo
                ]
                flux = pair_flux(own, across, 1, signs[l - 1])
                total = [t + v for t, v in zip(total, flux)]
            for f in range(nf):
                new = early[piece, f, x] + total[f]
                sec[piece, f, x] = sec[piece, f, x] + register_gain * total[f]
                mid = early[ch, f, x]
                reg_out[f, x, top, cols] = jnp.where(low, new, mid)
                reg_out[f, x, bottom, cols] = jnp.where(low, mid, new)

    def section_copies(p):
        return [
            remote(
                sec.at[p, :, pl.ds(0, 2)],
                srecv.at[p, 0],
                ss.at[p, 0],
                sr.at[p, 0],
                (prv, mine),
            ),
            remote(
                sec.at[p, :, pl.ds(nx - 2, 2)],
                srecv.at[p, 1],
                ss.at[p, 1],
                sr.at[p, 1],
                (nxt, mine),
            ),
        ]

    def chip_copies(p):
        return [
            remote(
                chip.at[p],
                chips.at[p, d - 1],
                cs.at[p, d - 1],
                cr.at[p, d - 1],
                (chip_peer(d), mine),
            )
            for d in range(1, zs)
        ]

    pieces = range(2 * n_ch)
    scopies = [section_copies(p) for p in pieces]
    abcopies = [
        remote(ab.at[p], pab.at[p], abs_.at[p], abr.at[p], (partner, mine)) for p in pieces
    ]
    ccopies = [chip_copies(p) for p in pieces]
    icopies = [
        remote(inc.at[p, core], pinc.at[p], ins.at[p], inr.at[p], (partner, mine))
        for p in pieces
    ]

    def begin(p):
        for f in range(nf):
            ahead = sec[p, f, 0]
            back = sec[p, f, nx - 1]
            for j in range(1, nx):
                ahead = sec[p, f, j] + mu * ahead
                back = sec[p, f, nx - 1 - j] + mu * back
            ab[p, 0, f] = ahead
            ab[p, 1, f] = back
        abcopies[p].start()
        for copy in scopies[p]:
            copy.start()

    def across_chips(p):
        abcopies[p].wait_recv()
        for f in range(nf):
            chip[p, f] = pab[p, core, f] + rho * ab[p, core, f]
        for copy in ccopies[p]:
            copy.start()

    def incoming(p):
        for copy in ccopies[p]:
            copy.wait_recv()
        scale = 1.0 / (1.0 - rho ** (2 * zs))
        for f in range(nf):
            total = (scale * rho ** (2 * (zs - 1))) * chip[p, f]
            for d in range(1, zs):
                total = total + (scale * rho ** (2 * (d - 1))) * chips[p, d - 1, f]
            inc[p, core, f] = total
        icopies[p].start()

    def finish(p):
        for copy in scopies[p]:
            copy.wait()
        icopies[p].wait()
        for f in range(nf):
            inc[p, 1 - core, f] = pab[p, 1 - core, f] + rho * pinc[p, f]
        for f in range(nf):
            s = (
                [srecv[p, 1, f, 0], srecv[p, 1, f, 1]]
                + [sec[p, f, j] for j in range(nx)]
                + [srecv[p, 0, f, 0], srecv[p, 0, f, 1]]
            )
            left = inc[p, 0, f]
            for j in range(nx):
                left = s[j + 2] + mu * left
                near = (
                    stencil[0] * s[j + 2]
                    + stencil[1] * (s[j + 1] + s[j + 3])
                    + stencil[2] * (s[j] + s[j + 4])
                )
                filt[p, f, j] = near + remainder * left
            right = inc[p, 1, f]
            for j in reversed(range(nx)):
                value = filt[p, f, j] + (remainder * mu) * right
                if p < n_ch:
                    filt[p, f, j] = value
                else:
                    mid = filt[p - n_ch, f, j]
                    cols = pl.ds((p - n_ch) * LANES, LANES)
                    filt_out[f, j, top, cols] = jnp.where(low, value, mid)
                    filt_out[f, j, bottom, cols] = jnp.where(low, mid, value)
                right = s[j + 2] + mu * right

    chunks = range(n_ch)

    for ch in chunks:
        x_pass(ch)
        begin(ch)
    for ch in chunks:
        across_chips(ch)
    for ch in chunks:
        y_pass(ch)
        begin(n_ch + ch)
        if ch == 0:
            for early_piece in chunks:
                incoming(early_piece)
        else:
            incoming(n_ch + ch - 1)
        across_chips(n_ch + ch)
    for p in range(2 * n_ch - 1):
        finish(p)
    incoming(2 * n_ch - 1)
    finish(2 * n_ch - 1)

    for ch in chunks:
        for copy in ycopies[ch]:
            copy.wait_send()
    for p in pieces:
        abcopies[p].wait_send()
        for copy in ccopies[p]:
            copy.wait_send()
    for copy in xcopies:
        copy.wait_send()


def body(n_gx, n_yz, state, register):
    nf, nx, ny, nz = state.shape
    n_ch = nz // LANES
    n_p = 2 * n_ch
    zs = n_gx // 2
    f32 = jnp.float32
    dma = pltpu.SemaphoreType.DMA
    return pl.pallas_call(
        functools.partial(kernel, n_gx, n_yz),
        out_shape=[jax.ShapeDtypeStruct(state.shape, f32)] * 2,
        in_specs=[pl.BlockSpec(memory_space=pl.ANY)] * 2,
        out_specs=[pl.BlockSpec(memory_space=pltpu.VMEM)] * 2,
        scratch_shapes=[
            pltpu.VMEM((nf, nx, ny, nz), f32),
            pltpu.VMEM((nf, nx, ny, nz), f32),
            pltpu.VMEM((6, nx + 8, ny, nz), f32),
            pltpu.VMEM((nf, nx, ny, nz), f32),
            pltpu.VMEM((2, nf, 4, ny, nz), f32),
            pltpu.VMEM((n_ch, 2, nf, nx, 4, LANES), f32),
            pltpu.VMEM((n_ch, 2, nf, nx, 4, LANES), f32),
            pltpu.VMEM((n_p, nf, nx, ROWS, LANES), f32),
            pltpu.VMEM((n_p, nf, nx, ROWS, LANES), f32),
            pltpu.VMEM((n_p, nf, nx, ROWS, LANES), f32),
            pltpu.VMEM((n_p, 2, nf, 2, ROWS, LANES), f32),
            pltpu.VMEM((n_p, 2, nf, ROWS, LANES), f32),
            pltpu.VMEM((n_p, 2, nf, ROWS, LANES), f32),
            pltpu.VMEM((n_p, nf, ROWS, LANES), f32),
            pltpu.VMEM((n_p, zs - 1, nf, ROWS, LANES), f32),
            pltpu.VMEM((n_p, 2, nf, ROWS, LANES), f32),
            pltpu.VMEM((n_p, nf, ROWS, LANES), f32),
            dma((2,)),
            dma((2,)),
            dma((n_ch, 2)),
            dma((n_ch, 2)),
            dma((n_p, 2)),
            dma((n_p, 2)),
            dma((n_p,)),
            dma((n_p,)),
            dma((n_p, zs - 1)),
            dma((n_p, zs - 1)),
            dma((n_p,)),
            dma((n_p,)),
            dma((2 * nf,)),
            pltpu.VMEM((nz, nz), jnp.bfloat16),
            pltpu.VMEM((n_products, nx * ny, nz), jnp.bfloat16),
            pltpu.VMEM((n_products, nx * ny, nz), jnp.bfloat16),
            pltpu.VMEM((n_products, nx * ny, nz), f32),
        ],
        compiler_params=pltpu.CompilerParams(
            collective_id=0, has_side_effects=True, vmem_limit_bytes=vmem_limit
        ),
    )(state, register)


def solution(mesh):
    spec = P(None, "gx", "yz", None)
    run = functools.partial(body, mesh.shape["gx"], mesh.shape["yz"])
    return jax.shard_map(
        lambda state, register: tuple(run(state, register)),
        mesh=mesh,
        in_specs=(spec, spec),
        out_specs=(spec, spec),
        check_vma=False,
    )
```

```python
import functools

import jax
import jax.numpy as jnp
from jax import lax
from jax.experimental import pallas as pl
from jax.experimental.pallas import tpu as pltpu
from jax.sharding import PartitionSpec as P

gamma_gas = 1.4
central_weights = (4.0 / 5.0, -1.0 / 5.0, 4.0 / 105.0, -1.0 / 280.0)
filter_alpha = 0.49
register_decay = -5.0 / 9.0
register_gain = 15.0 / 16.0
time_step = 0.2
MESH = pl.DeviceIdType.MESH
LANES = 128
ROWS = 8
n_products = 18
vmem_limit = 51 * 1024 * 1024


def filter_constants():
    alpha = filter_alpha
    a0 = (11.0 + 10.0 * alpha) / 16.0
    a1 = (15.0 + 34.0 * alpha) / 32.0
    a2 = (-3.0 + 6.0 * alpha) / 16.0
    a3 = (1.0 - 2.0 * alpha) / 32.0
    q2 = 4.0 * a3 / (2.0 * alpha)
    q1 = (2.0 * a2 - q2) / (2.0 * alpha)
    q0 = (a1 - 3.0 * a3 - q1) / (2.0 * alpha)
    rest = a0 - a2 - q0
    mu = (-1.0 + (1.0 - 4.0 * alpha * alpha) ** 0.5) / (2.0 * alpha)
    kappa = (1.0 + mu * mu) / (1.0 - mu * mu)
    return (q0 + 0.5 * q2, 0.5 * q1, 0.25 * q2), kappa * rest, mu


def split_products(fields):
    density, mom_x, mom_y, mom_z, energy = fields
    inverse = 1.0 / density
    u, v, w = mom_x * inverse, mom_y * inverse, mom_z * inverse
    pressure = (gamma_gas - 1.0) * (energy - 0.5 * (mom_x * u + mom_y * v + mom_z * w))
    total = energy + pressure
    h = total * inverse
    prims = [density, 0.5 * u, 0.5 * v, 0.5 * w, pressure, 0.5 * h]
    return prims, [
        density, w, mom_z,
        mom_z * u, w * u, mom_x, u,
        mom_z * v, w * v, mom_y, v,
        mom_z * w, w * w,
        mom_z * h, w * h, total, h,
        pressure,
    ]


def split_residual(prims, d, scale):
    density, u, v, w, _, h = prims
    u, v, w, h = u + u, v + v, w + w, h + h
    mom = density * w
    mass = d[2] + density * d[1] + w * d[0]

    def moment(q, d_mq, d_wq, d_rq, d_q):
        return scale * (d_mq + density * d_wq + w * d_rq + q * mass + mom * d_q)

    return [
        (2.0 * scale) * mass,
        moment(u, d[3], d[4], d[5], d[6]),
        moment(v, d[7], d[8], d[9], d[10]),
        moment(w, d[11], d[12], d[2], d[1]) + (4.0 * scale) * d[17],
        moment(h, d[13], d[14], d[15], d[16]),
    ]


def primitives(fields):
    density = fields[0]
    inverse = 1.0 / density
    speeds = [fields[i] * inverse for i in (1, 2, 3)]
    kinetic = 0.5 * (
        fields[1] * speeds[0] + fields[2] * speeds[1] + fields[3] * speeds[2]
    )
    pressure = (gamma_gas - 1.0) * (fields[4] - kinetic)
    enthalpy = (fields[4] + pressure) * (0.5 * inverse)
    return [density] + [0.5 * speed for speed in speeds] + [pressure, enthalpy]


def pair_flux(left, right, direction, weight):
    density, speed_x, speed_y, speed_z, pressure, enthalpy = [
        one + other for one, other in zip(left, right)
    ]
    normal = (speed_x, speed_y, speed_z)[direction]
    mass = (weight * density) * normal
    moment = [mass * speed_x, mass * speed_y, mass * speed_z]
    moment[direction] = moment[direction] + weight * pressure
    return [mass] + moment + [mass * enthalpy]


def kernel(
    n_gx,
    n_yz,
    state_in,
    register_in,
    reg_out,
    filt_out,
    state,
    register,
    prims,
    acc,
    xrecv,
    ysend,
    yrecv,
    sec,
    early,
    filt,
    srecv,
    ab,
    pab,
    chip,
    chips,
    inc,
    pinc,
    xs,
    xr,
    ys,
    yr,
    ss,
    sr,
    abs_,
    abr,
    cs,
    cr,
    ins,
    inr,
    local,
    matrix,
    high,
    rest,
    deriv,
):
    nf, nx, ny, nz = state.shape
    n_ch = nz // LANES
    tiles = ny // ROWS
    zs = n_gx // 2
    me = lax.axis_index("gx")
    mine = lax.axis_index("yz")
    core = lax.rem(me, 2)
    chip_at = lax.div(me, 2)
    nxt = lax.rem(me + 1, n_gx)
    prv = lax.rem(me + n_gx - 1, n_gx)
    partner = me + 1 - 2 * core
    ynxt = lax.rem(mine + 1, n_yz)
    yprv = lax.rem(mine + n_yz - 1, n_yz)

    def chip_peer(d):
        return 2 * lax.rem(chip_at + (1 - 2 * core) * d + zs, zs) + core

    barrier = pltpu.get_barrier_semaphore()
    peers = [(prv, mine), (nxt, mine), (me, yprv), (me, ynxt)]
    peers += [(chip_peer(d), mine) for d in range(1, zs)]
    for peer in peers:
        pl.semaphore_signal(barrier, inc=1, device_id=peer, device_id_type=MESH)

    loads = [
        pltpu.make_async_copy(state_in.at[f], state.at[f], local.at[f]) for f in range(nf)
    ]
    loads += [
        pltpu.make_async_copy(register_in.at[f], register.at[f], local.at[nf + f])
        for f in range(nf)
    ]
    for load in loads:
        load.start()

    gap = lax.broadcasted_iota(jnp.int32, (nz, nz), 0) - lax.broadcasted_iota(
        jnp.int32, (nz, nz), 1
    )
    gap = jnp.where(gap < 0, gap + nz, gap)
    entries = jnp.zeros((nz, nz), jnp.float32)
    for l in range(1, 5):
        whole = float(round(840.0 * central_weights[l - 1]))
        entries = jnp.where(gap == l, whole, jnp.where(gap == nz - l, -whole, entries))
    matrix[...] = entries.astype(jnp.bfloat16)

    for f in range(nf):
        loads[f].wait()

        @pl.loop(0, nx, unroll=4)
        def _(x, f=f):
            for ch in range(n_ch):
                cols = pl.ds(ch * LANES, LANES)
                ysend[ch, 0, f, x] = state[f, x, pl.ds(0, ROWS), cols][:4]
                ysend[ch, 1, f, x] = state[f, x, pl.ds(ny - ROWS, ROWS), cols][4:]

    pl.semaphore_wait(barrier, len(peers))

    def remote(src, dst, send, recv, peer):
        return pltpu.make_async_remote_copy(
            src_ref=src,
            dst_ref=dst,
            send_sem=send,
            recv_sem=recv,
            device_id=peer,
            device_id_type=MESH,
        )

    def y_copies(ch):
        return [
            remote(
                ysend.at[ch, side, f],
                yrecv.at[ch, side, f],
                ys.at[ch, side, f],
                yr.at[ch, side, f],
                (me, (yprv, ynxt)[side]),
            )
            for f in range(nf)
            for side in range(2)
        ]

    ycopies = [y_copies(ch) for ch in range(n_ch)]
    xcopies = [
        remote(
            state.at[f, pl.ds((0, nx - 4)[side], 4)],
            xrecv.at[side, f],
            xs.at[side, f],
            xr.at[side, f],
            ((prv, nxt)[side], mine),
        )
        for f in range(nf)
        for side in range(2)
    ]
    for ycopy, xcopy in zip(ycopies[0], xcopies):
        ycopy.start()
        xcopy.start()
    for ch in range(1, n_ch):
        for copy in ycopies[ch]:
            copy.start()

    weights = [-time_step * w for w in central_weights]

    @pl.loop(0, nx)
    def _(x):
        rows = pl.ds(pl.multiple_of(x * ny, ny), ny)
        own, products = split_products([state[f, x] for f in range(nf)])
        for f in range(6):
            prims[f, x + 4] = own[f]
        for k, value in enumerate(products):
            part = value.astype(jnp.bfloat16)
            high[k, rows, :] = part
            rest[k, rows, :] = (value - part.astype(jnp.float32)).astype(jnp.bfloat16)

    @pl.loop(0, n_products)
    def _(k):
        whole = jnp.dot(high[k], matrix[...], preferred_element_type=jnp.float32)
        deriv[k] = whole + jnp.dot(rest[k], matrix[...], preferred_element_type=jnp.float32)

    @pl.loop(0, nx * tiles)
    def _(i):
        x = i // tiles
        rows = pl.ds(pl.multiple_of((i % tiles) * ROWS, ROWS), ROWS)
        flat = pl.ds(pl.multiple_of(i * ROWS, ROWS), ROWS)
        total = split_residual(
            [prims[f, x + 4, rows, :] for f in range(6)],
            [deriv[k, flat, :] for k in range(n_products)],
            -time_step / (4.0 * 840.0),
        )
        for f in range(nf):
            acc[f, x, rows, :] = total[f]

    place = lax.broadcasted_iota(jnp.int32, (ny, LANES), 0)

    @pl.loop(0, nx)
    def _(x):
        for ch in range(n_ch):
            cols = pl.ds(ch * LANES, LANES)
            own = [prims[f, x + 4, :, cols] for f in range(6)]
            total = [acc[f, x, :, cols] for f in range(nf)]
            for l in range(1, 5):
                ahead = [pltpu.roll(q, ny - l, axis=0) for q in own]
                inside = jnp.where(place < ny - l, weights[l - 1], 0.0)
                flux = pair_flux(own, ahead, 1, inside)
                total = [t + (v - pltpu.roll(v, l, axis=0)) for t, v in zip(total, flux)]
            for f in range(nf):
                acc[f, x, :, cols] = total[f]

    for copy in xcopies:
        copy.wait_recv()

    @pl.loop(0, 4 * tiles)
    def _(i):
        x = i // tiles
        rows = pl.ds(pl.multiple_of((i % tiles) * ROWS, ROWS), ROWS)
        for side in range(2):
            got = primitives([xrecv[side, f, x, rows, :] for f in range(nf)])
            for f in range(6):
                prims[f, x + (nx + 4, 0)[side], rows, :] = got[f]

    for load in loads[nf:]:
        load.wait()

    stencil, remainder, mu = filter_constants()
    rho = mu**nx
    low = lax.broadcasted_iota(jnp.int32, (ROWS, LANES), 0) < 4
    top, bottom = pl.ds(0, ROWS), pl.ds(ny - ROWS, ROWS)

    def inner(first, last):
        return jnp.where(low, last, first)

    def outer(first, last):
        return jnp.where(low, first, last)

    def x_pass(ch):
        cols = pl.ds(ch * LANES, LANES)

        @pl.loop(0, nx)
        def _(x):
            parts = []
            for rows in (top, bottom):
                own = [prims[f, x + 4, rows, cols] for f in range(6)]
                total = [acc[f, x, rows, cols] for f in range(nf)]
                for l in range(1, 5):
                    ahead = [prims[f, x + 4 + l, rows, cols] for f in range(6)]
                    behind = [prims[f, x + 4 - l, rows, cols] for f in range(6)]
                    up = pair_flux(own, ahead, 0, weights[l - 1])
                    down = pair_flux(behind, own, 0, weights[l - 1])
                    total = [t + (u - d) for t, u, d in zip(total, up, down)]
                parts.append(
                    [
                        register_decay * register[f, x, rows, cols] + total[f]
                        for f in range(nf)
                    ]
                )
            for f in range(nf):
                first, last = parts[0][f], parts[1][f]
                state_first, state_last = state[f, x, top, cols], state[f, x, bottom, cols]
                for piece, pick in ((ch, inner), (n_ch + ch, outer)):
                    value = pick(first, last)
                    early[piece, f, x] = value
                    sec[piece, f, x] = pick(state_first, state_last) + register_gain * value

    signs = []
    spot = lax.broadcasted_iota(jnp.int32, (ROWS, LANES), 0)
    for l in range(1, 5):
        w = weights[l - 1]
        signs.append(jnp.where(spot < l, -w, jnp.where(spot >= ROWS - l, w, 0.0)))

    def y_pass(ch):
        piece = n_ch + ch
        cols = pl.ds(ch * LANES, LANES)
        for copy in ycopies[ch]:
            copy.wait_recv()

        @pl.loop(0, nx, unroll=2)
        def _(x):
            halo = primitives(
                [
                    jnp.concatenate([yrecv[ch, 0, f, x], yrecv[ch, 1, f, x]], axis=0)
                    for f in range(nf)
                ]
            )
            own = [
                outer(prims[f, x + 4, top, cols], prims[f, x + 4, bottom, cols])
                for f in range(6)
            ]
            total = [jnp.zeros((ROWS, LANES), jnp.float32) for _ in range(nf)]
            for l in range(1, 5):
                across = [
                    jnp.where(low, pltpu.roll(q, l, axis=0), pltpu.roll(q, ROWS - l, axis=0))
                    if l < 4
                    else pltpu.roll(q, l, axis=0)
                    for q in halo
                ]
                flux = pair_flux(own, across, 1, signs[l - 1])
                total = [t + v for t, v in zip(total, flux)]
            for f in range(nf):
                new = early[piece, f, x] + total[f]
                sec[piece, f, x] = sec[piece, f, x] + register_gain * total[f]
                mid = early[ch, f, x]
                reg_out[f, x, top, cols] = jnp.where(low, new, mid)
                reg_out[f, x, bottom, cols] = jnp.where(low, mid, new)

    def section_copies(p):
        return [
            remote(
                sec.at[p, :, pl.ds(0, 2)],
                srecv.at[p, 0],
                ss.at[p, 0],
                sr.at[p, 0],
                (prv, mine),
            ),
            remote(
                sec.at[p, :, pl.ds(nx - 2, 2)],
                srecv.at[p, 1],
                ss.at[p, 1],
                sr.at[p, 1],
                (nxt, mine),
            ),
        ]

    def chip_copies(p):
        return [
            remote(
                chip.at[p],
                chips.at[p, d - 1],
                cs.at[p, d - 1],
                cr.at[p, d - 1],
                (chip_peer(d), mine),
            )
            for d in range(1, zs)
        ]

    pieces = range(2 * n_ch)
    scopies = [section_copies(p) for p in pieces]
    abcopies = [
        remote(ab.at[p], pab.at[p], abs_.at[p], abr.at[p], (partner, mine)) for p in pieces
    ]
    ccopies = [chip_copies(p) for p in pieces]
    icopies = [
        remote(inc.at[p, core], pinc.at[p], ins.at[p], inr.at[p], (partner, mine))
        for p in pieces
    ]

    def begin(p):
        for f in range(nf):
            ahead = sec[p, f, 0]
            back = sec[p, f, nx - 1]
            for j in range(1, nx):
                ahead = sec[p, f, j] + mu * ahead
                back = sec[p, f, nx - 1 - j] + mu * back
            ab[p, 0, f] = ahead
            ab[p, 1, f] = back
        abcopies[p].start()
        for copy in scopies[p]:
            copy.start()

    def across_chips(p):
        abcopies[p].wait_recv()
        for f in range(nf):
            chip[p, f] = pab[p, core, f] + rho * ab[p, core, f]
        for copy in ccopies[p]:
            copy.start()

    def incoming(p):
        for copy in ccopies[p]:
            copy.wait_recv()
        scale = 1.0 / (1.0 - rho ** (2 * zs))
        for f in range(nf):
            total = (scale * rho ** (2 * (zs - 1))) * chip[p, f]
            for d in range(1, zs):
                total = total + (scale * rho ** (2 * (d - 1))) * chips[p, d - 1, f]
            inc[p, core, f] = total
        icopies[p].start()

    def finish(p):
        for copy in scopies[p]:
            copy.wait()
        icopies[p].wait()
        for f in range(nf):
            inc[p, 1 - core, f] = pab[p, 1 - core, f] + rho * pinc[p, f]
        for f in range(nf):
            s = (
                [srecv[p, 1, f, 0], srecv[p, 1, f, 1]]
                + [sec[p, f, j] for j in range(nx)]
                + [srecv[p, 0, f, 0], srecv[p, 0, f, 1]]
            )
            left = inc[p, 0, f]
            for j in range(nx):
                left = s[j + 2] + mu * left
                near = (
                    stencil[0] * s[j + 2]
                    + stencil[1] * (s[j + 1] + s[j + 3])
                    + stencil[2] * (s[j] + s[j + 4])
                )
                filt[p, f, j] = near + remainder * left
            right = inc[p, 1, f]
            for j in reversed(range(nx)):
                value = filt[p, f, j] + (remainder * mu) * right
                if p < n_ch:
                    filt[p, f, j] = value
                else:
                    mid = filt[p - n_ch, f, j]
                    cols = pl.ds((p - n_ch) * LANES, LANES)
                    filt_out[f, j, top, cols] = jnp.where(low, value, mid)
                    filt_out[f, j, bottom, cols] = jnp.where(low, mid, value)
                right = s[j + 2] + mu * right

    chunks = range(n_ch)

    for ch in chunks:
        x_pass(ch)
        begin(ch)
    for ch in chunks:
        across_chips(ch)
    for ch in chunks:
        y_pass(ch)
        begin(n_ch + ch)
        if ch == 0:
            for early_piece in chunks:
                incoming(early_piece)
        else:
            incoming(n_ch + ch - 1)
        across_chips(n_ch + ch)
    for p in range(2 * n_ch - 1):
        finish(p)
    incoming(2 * n_ch - 1)
    finish(2 * n_ch - 1)

    for ch in chunks:
        for copy in ycopies[ch]:
            copy.wait_send()
    for p in pieces:
        abcopies[p].wait_send()
        for copy in ccopies[p]:
            copy.wait_send()
    for copy in xcopies:
        copy.wait_send()


def body(n_gx, n_yz, state, register):
    nf, nx, ny, nz = state.shape
    n_ch = nz // LANES
    n_p = 2 * n_ch
    zs = n_gx // 2
    f32 = jnp.float32
    dma = pltpu.SemaphoreType.DMA
    return pl.pallas_call(
        functools.partial(kernel, n_gx, n_yz),
        out_shape=[jax.ShapeDtypeStruct(state.shape, f32)] * 2,
        in_specs=[pl.BlockSpec(memory_space=pl.ANY)] * 2,
        out_specs=[pl.BlockSpec(memory_space=pltpu.VMEM)] * 2,
        scratch_shapes=[
            pltpu.VMEM((nf, nx, ny, nz), f32),
            pltpu.VMEM((nf, nx, ny, nz), f32),
            pltpu.VMEM((6, nx + 8, ny, nz), f32),
            pltpu.VMEM((nf, nx, ny, nz), f32),
            pltpu.VMEM((2, nf, 4, ny, nz), f32),
            pltpu.VMEM((n_ch, 2, nf, nx, 4, LANES), f32),
            pltpu.VMEM((n_ch, 2, nf, nx, 4, LANES), f32),
            pltpu.VMEM((n_p, nf, nx, ROWS, LANES), f32),
            pltpu.VMEM((n_p, nf, nx, ROWS, LANES), f32),
            pltpu.VMEM((n_p, nf, nx, ROWS, LANES), f32),
            pltpu.VMEM((n_p, 2, nf, 2, ROWS, LANES), f32),
            pltpu.VMEM((n_p, 2, nf, ROWS, LANES), f32),
            pltpu.VMEM((n_p, 2, nf, ROWS, LANES), f32),
            pltpu.VMEM((n_p, nf, ROWS, LANES), f32),
            pltpu.VMEM((n_p, zs - 1, nf, ROWS, LANES), f32),
            pltpu.VMEM((n_p, 2, nf, ROWS, LANES), f32),
            pltpu.VMEM((n_p, nf, ROWS, LANES), f32),
            dma((2, nf)),
            dma((2, nf)),
            dma((n_ch, 2, nf)),
            dma((n_ch, 2, nf)),
            dma((n_p, 2)),
            dma((n_p, 2)),
            dma((n_p,)),
            dma((n_p,)),
            dma((n_p, zs - 1)),
            dma((n_p, zs - 1)),
            dma((n_p,)),
            dma((n_p,)),
            dma((2 * nf,)),
            pltpu.VMEM((nz, nz), jnp.bfloat16),
            pltpu.VMEM((n_products, nx * ny, nz), jnp.bfloat16),
            pltpu.VMEM((n_products, nx * ny, nz), jnp.bfloat16),
            pltpu.VMEM((n_products, nx * ny, nz), f32),
        ],
        compiler_params=pltpu.CompilerParams(
            collective_id=0, has_side_effects=True, vmem_limit_bytes=vmem_limit
        ),
    )(state, register)


def solution(mesh):
    spec = P(None, "gx", "yz", None)
    run = functools.partial(body, mesh.shape["gx"], mesh.shape["yz"])
    return jax.shard_map(
        lambda state, register: tuple(run(state, register)),
        mesh=mesh,
        in_specs=(spec, spec),
        out_specs=(spec, spec),
        check_vma=False,
    )
```

```python
import functools

import jax
import jax.numpy as jnp
from jax import lax
from jax.experimental import pallas as pl
from jax.experimental.pallas import tpu as pltpu
from jax.sharding import PartitionSpec as P

gamma_gas = 1.4
central_weights = (4.0 / 5.0, -1.0 / 5.0, 4.0 / 105.0, -1.0 / 280.0)
filter_alpha = 0.49
register_decay = -5.0 / 9.0
register_gain = 15.0 / 16.0
time_step = 0.2
MESH = pl.DeviceIdType.MESH
LANES = 128
ROWS = 8
n_products = 18
vmem_limit = 51 * 1024 * 1024


def filter_constants():
    alpha = filter_alpha
    a0 = (11.0 + 10.0 * alpha) / 16.0
    a1 = (15.0 + 34.0 * alpha) / 32.0
    a2 = (-3.0 + 6.0 * alpha) / 16.0
    a3 = (1.0 - 2.0 * alpha) / 32.0
    q2 = 4.0 * a3 / (2.0 * alpha)
    q1 = (2.0 * a2 - q2) / (2.0 * alpha)
    q0 = (a1 - 3.0 * a3 - q1) / (2.0 * alpha)
    rest = a0 - a2 - q0
    mu = (-1.0 + (1.0 - 4.0 * alpha * alpha) ** 0.5) / (2.0 * alpha)
    kappa = (1.0 + mu * mu) / (1.0 - mu * mu)
    return (q0 + 0.5 * q2, 0.5 * q1, 0.25 * q2), kappa * rest, mu


def split_products(fields):
    density, mom_x, mom_y, mom_z, energy = fields
    inverse = 1.0 / density
    u, v, w = mom_x * inverse, mom_y * inverse, mom_z * inverse
    pressure = (gamma_gas - 1.0) * (energy - 0.5 * (mom_x * u + mom_y * v + mom_z * w))
    total = energy + pressure
    h = total * inverse
    prims = [density, 0.5 * u, 0.5 * v, 0.5 * w, pressure, 0.5 * h]
    return prims, [
        density, w, mom_z,
        mom_z * u, w * u, mom_x, u,
        mom_z * v, w * v, mom_y, v,
        mom_z * w, w * w,
        mom_z * h, w * h, total, h,
        pressure,
    ]


def split_residual(prims, d, scale):
    density, u, v, w, _, h = prims
    u, v, w, h = u + u, v + v, w + w, h + h
    mom = density * w
    mass = d[2] + density * d[1] + w * d[0]

    def moment(q, d_mq, d_wq, d_rq, d_q):
        return scale * (d_mq + density * d_wq + w * d_rq + q * mass + mom * d_q)

    return [
        (2.0 * scale) * mass,
        moment(u, d[3], d[4], d[5], d[6]),
        moment(v, d[7], d[8], d[9], d[10]),
        moment(w, d[11], d[12], d[2], d[1]) + (4.0 * scale) * d[17],
        moment(h, d[13], d[14], d[15], d[16]),
    ]


def primitives(fields):
    density = fields[0]
    inverse = 1.0 / density
    speeds = [fields[i] * inverse for i in (1, 2, 3)]
    kinetic = 0.5 * (
        fields[1] * speeds[0] + fields[2] * speeds[1] + fields[3] * speeds[2]
    )
    pressure = (gamma_gas - 1.0) * (fields[4] - kinetic)
    enthalpy = (fields[4] + pressure) * (0.5 * inverse)
    return [density] + [0.5 * speed for speed in speeds] + [pressure, enthalpy]


def pair_flux(left, right, direction, weight):
    density, speed_x, speed_y, speed_z, pressure, enthalpy = [
        one + other for one, other in zip(left, right)
    ]
    normal = (speed_x, speed_y, speed_z)[direction]
    mass = (weight * density) * normal
    moment = [mass * speed_x, mass * speed_y, mass * speed_z]
    moment[direction] = moment[direction] + weight * pressure
    return [mass] + moment + [mass * enthalpy]


def line_pass(low, high, first, last, direction, weights, get, put):
    held, totals = {}, {}
    for a in range(low, last):
        for b in range(a, min(a + 5, high)):
            if b not in held:
                held[b] = get(b)
        for l in range(1, 5):
            b = a + l
            if b >= high or (a < first and not first <= b < last):
                continue
            flux = pair_flux(held[a], held[b], direction, weights[l - 1])
            if a >= first:
                totals[a] = [t + v for t, v in zip(totals[a], flux)] if a in totals else flux
            if first <= b < last:
                totals[b] = (
                    [t - v for t, v in zip(totals[b], flux)]
                    if b in totals
                    else [-v for v in flux]
                )
        if a >= first:
            put(a, totals.pop(a))
        held.pop(a)


def kernel(
    n_gx,
    n_yz,
    state_in,
    register_in,
    reg_out,
    filt_out,
    state,
    register,
    prims,
    acc,
    xrecv,
    ysend,
    yrecv,
    sec,
    early,
    filt,
    srecv,
    ab,
    pab,
    chip,
    chips,
    inc,
    pinc,
    xs,
    xr,
    ys,
    yr,
    ss,
    sr,
    abs_,
    abr,
    cs,
    cr,
    ins,
    inr,
    local,
    matrix,
    high,
    rest,
    deriv,
    yprims,
    yacc,
):
    nf, nx, ny, nz = state.shape
    n_ch = nz // LANES
    tiles = ny // ROWS
    zs = n_gx // 2
    me = lax.axis_index("gx")
    mine = lax.axis_index("yz")
    core = lax.rem(me, 2)
    chip_at = lax.div(me, 2)
    nxt = lax.rem(me + 1, n_gx)
    prv = lax.rem(me + n_gx - 1, n_gx)
    partner = me + 1 - 2 * core
    ynxt = lax.rem(mine + 1, n_yz)
    yprv = lax.rem(mine + n_yz - 1, n_yz)

    def chip_peer(d):
        return 2 * lax.rem(chip_at + (1 - 2 * core) * d + zs, zs) + core

    barrier = pltpu.get_barrier_semaphore()
    peers = [(prv, mine), (nxt, mine), (me, yprv), (me, ynxt)]
    peers += [(chip_peer(d), mine) for d in range(1, zs)]
    for peer in peers:
        pl.semaphore_signal(barrier, inc=1, device_id=peer, device_id_type=MESH)

    loads = [
        pltpu.make_async_copy(state_in.at[f], state.at[f], local.at[f]) for f in range(nf)
    ]
    loads += [
        pltpu.make_async_copy(register_in.at[f], register.at[f], local.at[nf + f])
        for f in range(nf)
    ]
    for load in loads:
        load.start()

    gap = lax.broadcasted_iota(jnp.int32, (nz, nz), 0) - lax.broadcasted_iota(
        jnp.int32, (nz, nz), 1
    )
    gap = jnp.where(gap < 0, gap + nz, gap)
    entries = jnp.zeros((nz, nz), jnp.float32)
    for l in range(1, 5):
        whole = float(round(840.0 * central_weights[l - 1]))
        entries = jnp.where(gap == l, whole, jnp.where(gap == nz - l, -whole, entries))
    matrix[...] = entries.astype(jnp.bfloat16)

    for f in range(nf):
        loads[f].wait()

        @pl.loop(0, nx, unroll=4)
        def _(x, f=f):
            for ch in range(n_ch):
                cols = pl.ds(ch * LANES, LANES)
                ysend[ch, 0, f, x] = state[f, x, pl.ds(0, ROWS), cols][:4]
                ysend[ch, 1, f, x] = state[f, x, pl.ds(ny - ROWS, ROWS), cols][4:]

    pl.semaphore_wait(barrier, len(peers))

    def remote(src, dst, send, recv, peer):
        return pltpu.make_async_remote_copy(
            src_ref=src,
            dst_ref=dst,
            send_sem=send,
            recv_sem=recv,
            device_id=peer,
            device_id_type=MESH,
        )

    def y_copies(ch):
        return [
            remote(
                ysend.at[ch, side, f],
                yrecv.at[ch, side, f],
                ys.at[ch, side, f],
                yr.at[ch, side, f],
                (me, (yprv, ynxt)[side]),
            )
            for f in range(nf)
            for side in range(2)
        ]

    ycopies = [y_copies(ch) for ch in range(n_ch)]
    xcopies = [
        remote(
            state.at[f, pl.ds((0, nx - 4)[side], 4)],
            xrecv.at[side, f],
            xs.at[side, f],
            xr.at[side, f],
            ((prv, nxt)[side], mine),
        )
        for f in range(nf)
        for side in range(2)
    ]
    for ycopy, xcopy in zip(ycopies[0], xcopies):
        ycopy.start()
        xcopy.start()
    for ch in range(1, n_ch):
        for copy in ycopies[ch]:
            copy.start()

    weights = [-time_step * w for w in central_weights]

    @pl.loop(0, nx)
    def _(x):
        rows = pl.ds(pl.multiple_of(x * ny, ny), ny)
        own, products = split_products([state[f, x] for f in range(nf)])
        for f in range(6):
            prims[f, x + 4] = own[f]
            for ch in range(n_ch):
                yprims[f, ch, rows, :] = own[f][:, ch * LANES : (ch + 1) * LANES]
        for k, value in enumerate(products):
            part = value.astype(jnp.bfloat16)
            high[k, rows, :] = part
            rest[k, rows, :] = (value - part.astype(jnp.float32)).astype(jnp.bfloat16)

    @pl.loop(0, n_products)
    def _(k):
        whole = jnp.dot(high[k], matrix[...], preferred_element_type=jnp.float32)
        deriv[k] = whole + jnp.dot(rest[k], matrix[...], preferred_element_type=jnp.float32)

    @pl.loop(0, nx * tiles)
    def _(i):
        x = i // tiles
        rows = pl.ds(pl.multiple_of((i % tiles) * ROWS, ROWS), ROWS)
        flat = pl.ds(pl.multiple_of(i * ROWS, ROWS), ROWS)
        total = split_residual(
            [prims[f, x + 4, rows, :] for f in range(6)],
            [deriv[k, flat, :] for k in range(n_products)],
            -time_step / (4.0 * 840.0),
        )
        for f in range(nf):
            acc[f, x, rows, :] = total[f]

    @pl.loop(0, n_ch * (nx // ROWS))
    def _(i):
        ch = i // (nx // ROWS)
        base = (i % (nx // ROWS)) * (ROWS * ny)

        def at(y):
            return pl.ds(base + y, ROWS, stride=ny)

        line_pass(
            0,
            ny,
            0,
            ny,
            1,
            weights,
            lambda y: [yprims[f, ch, at(y), :] for f in range(6)],
            lambda y, total: [
                yacc.__setitem__((f, ch, at(y), slice(None)), total[f]) for f in range(nf)
            ],
        )

    for copy in xcopies:
        copy.wait_recv()

    @pl.loop(0, 4 * tiles)
    def _(i):
        x = i // tiles
        rows = pl.ds(pl.multiple_of((i % tiles) * ROWS, ROWS), ROWS)
        for side in range(2):
            got = primitives([xrecv[side, f, x, rows, :] for f in range(nf)])
            for f in range(6):
                prims[f, x + (nx + 4, 0)[side], rows, :] = got[f]

    for load in loads[nf:]:
        load.wait()

    stencil, remainder, mu = filter_constants()
    rho = mu**nx
    low = lax.broadcasted_iota(jnp.int32, (ROWS, LANES), 0) < 4
    top, bottom = pl.ds(0, ROWS), pl.ds(ny - ROWS, ROWS)

    def inner(first, last):
        return jnp.where(low, last, first)

    def outer(first, last):
        return jnp.where(low, first, last)

    def x_pass(ch):
        cols = pl.ds(ch * LANES, LANES)

        @pl.loop(0, tiles)
        def _(i):
            rows = pl.ds(pl.multiple_of(i * ROWS, ROWS), ROWS)

            def put(x, total):
                for f in range(nf):
                    acc[f, x, rows, cols] = acc[f, x, rows, cols] + total[f]

            line_pass(
                -4,
                nx + 4,
                0,
                nx,
                0,
                weights,
                lambda x: [prims[f, x + 4, rows, cols] for f in range(6)],
                put,
            )

        @pl.loop(0, nx, unroll=2)
        def _(x):
            for f in range(nf):
                ends = []
                for k, rows in enumerate((top, bottom)):
                    flat = pl.ds(pl.multiple_of(x * ny + k * (ny - ROWS), ROWS), ROWS)
                    ends.append(
                        register_decay * register[f, x, rows, cols]
                        + (acc[f, x, rows, cols] + yacc[f, ch, flat, :])
                    )
                first, last = ends
                state_first, state_last = state[f, x, top, cols], state[f, x, bottom, cols]
                for piece, pick in ((ch, inner), (n_ch + ch, outer)):
                    value = pick(first, last)
                    early[piece, f, x] = value
                    sec[piece, f, x] = pick(state_first, state_last) + register_gain * value

    signs = []
    spot = lax.broadcasted_iota(jnp.int32, (ROWS, LANES), 0)
    for l in range(1, 5):
        w = weights[l - 1]
        signs.append(jnp.where(spot < l, -w, jnp.where(spot >= ROWS - l, w, 0.0)))

    def y_pass(ch):
        piece = n_ch + ch
        cols = pl.ds(ch * LANES, LANES)
        for copy in ycopies[ch]:
            copy.wait_recv()

        @pl.loop(0, nx, unroll=2)
        def _(x):
            halo = primitives(
                [
                    jnp.concatenate([yrecv[ch, 0, f, x], yrecv[ch, 1, f, x]], axis=0)
                    for f in range(nf)
                ]
            )
            own = [
                outer(prims[f, x + 4, top, cols], prims[f, x + 4, bottom, cols])
                for f in range(6)
            ]
            total = [jnp.zeros((ROWS, LANES), jnp.float32) for _ in range(nf)]
            for l in range(1, 5):
                across = [
                    jnp.where(low, pltpu.roll(q, l, axis=0), pltpu.roll(q, ROWS - l, axis=0))
                    if l < 4
                    else pltpu.roll(q, l, axis=0)
                    for q in halo
                ]
                flux = pair_flux(own, across, 1, signs[l - 1])
                total = [t + v for t, v in zip(total, flux)]
            for f in range(nf):
                new = early[piece, f, x] + total[f]
                sec[piece, f, x] = sec[piece, f, x] + register_gain * total[f]
                mid = early[ch, f, x]
                reg_out[f, x, top, cols] = jnp.where(low, new, mid)
                reg_out[f, x, bottom, cols] = jnp.where(low, mid, new)

    def section_copies(p):
        return [
            remote(
                sec.at[p, :, pl.ds(0, 2)],
                srecv.at[p, 0],
                ss.at[p, 0],
                sr.at[p, 0],
                (prv, mine),
            ),
            remote(
                sec.at[p, :, pl.ds(nx - 2, 2)],
                srecv.at[p, 1],
                ss.at[p, 1],
                sr.at[p, 1],
                (nxt, mine),
            ),
        ]

    def chip_copies(p):
        return [
            remote(
                chip.at[p],
                chips.at[p, d - 1],
                cs.at[p, d - 1],
                cr.at[p, d - 1],
                (chip_peer(d), mine),
            )
            for d in range(1, zs)
        ]

    pieces = range(2 * n_ch)
    scopies = [section_copies(p) for p in pieces]
    abcopies = [
        remote(ab.at[p], pab.at[p], abs_.at[p], abr.at[p], (partner, mine)) for p in pieces
    ]
    ccopies = [chip_copies(p) for p in pieces]
    icopies = [
        remote(inc.at[p, core], pinc.at[p], ins.at[p], inr.at[p], (partner, mine))
        for p in pieces
    ]

    def begin(p):
        for f in range(nf):
            ahead = sec[p, f, 0]
            back = sec[p, f, nx - 1]
            for j in range(1, nx):
                ahead = sec[p, f, j] + mu * ahead
                back = sec[p, f, nx - 1 - j] + mu * back
            ab[p, 0, f] = ahead
            ab[p, 1, f] = back
        abcopies[p].start()
        for copy in scopies[p]:
            copy.start()

    def across_chips(p):
        abcopies[p].wait_recv()
        for f in range(nf):
            chip[p, f] = pab[p, core, f] + rho * ab[p, core, f]
        for copy in ccopies[p]:
            copy.start()

    def incoming(p):
        for copy in ccopies[p]:
            copy.wait_recv()
        scale = 1.0 / (1.0 - rho ** (2 * zs))
        for f in range(nf):
            total = (scale * rho ** (2 * (zs - 1))) * chip[p, f]
            for d in range(1, zs):
                total = total + (scale * rho ** (2 * (d - 1))) * chips[p, d - 1, f]
            inc[p, core, f] = total
        icopies[p].start()

    def finish(p):
        for copy in scopies[p]:
            copy.wait()
        icopies[p].wait()
        for f in range(nf):
            inc[p, 1 - core, f] = pab[p, 1 - core, f] + rho * pinc[p, f]
        for f in range(nf):
            s = (
                [srecv[p, 1, f, 0], srecv[p, 1, f, 1]]
                + [sec[p, f, j] for j in range(nx)]
                + [srecv[p, 0, f, 0], srecv[p, 0, f, 1]]
            )
            left = inc[p, 0, f]
            for j in range(nx):
                left = s[j + 2] + mu * left
                near = (
                    stencil[0] * s[j + 2]
                    + stencil[1] * (s[j + 1] + s[j + 3])
                    + stencil[2] * (s[j] + s[j + 4])
                )
                filt[p, f, j] = near + remainder * left
            right = inc[p, 1, f]
            for j in reversed(range(nx)):
                value = filt[p, f, j] + (remainder * mu) * right
                if p < n_ch:
                    filt[p, f, j] = value
                else:
                    mid = filt[p - n_ch, f, j]
                    cols = pl.ds((p - n_ch) * LANES, LANES)
                    filt_out[f, j, top, cols] = jnp.where(low, value, mid)
                    filt_out[f, j, bottom, cols] = jnp.where(low, mid, value)
                right = s[j + 2] + mu * right

    chunks = range(n_ch)

    for ch in chunks:
        x_pass(ch)
        begin(ch)
    for ch in chunks:
        across_chips(ch)
    for ch in chunks:
        y_pass(ch)
        begin(n_ch + ch)
        if ch == 0:
            for early_piece in chunks:
                incoming(early_piece)
        else:
            incoming(n_ch + ch - 1)
        across_chips(n_ch + ch)
    for p in range(2 * n_ch - 1):
        finish(p)
    incoming(2 * n_ch - 1)
    finish(2 * n_ch - 1)

    for ch in chunks:
        for copy in ycopies[ch]:
            copy.wait_send()
    for p in pieces:
        abcopies[p].wait_send()
        for copy in ccopies[p]:
            copy.wait_send()
    for copy in xcopies:
        copy.wait_send()


def body(n_gx, n_yz, state, register):
    nf, nx, ny, nz = state.shape
    n_ch = nz // LANES
    n_p = 2 * n_ch
    zs = n_gx // 2
    f32 = jnp.float32
    dma = pltpu.SemaphoreType.DMA
    return pl.pallas_call(
        functools.partial(kernel, n_gx, n_yz),
        out_shape=[jax.ShapeDtypeStruct(state.shape, f32)] * 2,
        in_specs=[pl.BlockSpec(memory_space=pl.ANY)] * 2,
        out_specs=[pl.BlockSpec(memory_space=pltpu.VMEM)] * 2,
        scratch_shapes=[
            pltpu.VMEM((nf, nx, ny, nz), f32),
            pltpu.VMEM((nf, nx, ny, nz), f32),
            pltpu.VMEM((6, nx + 8, ny, nz), f32),
            pltpu.VMEM((nf, nx, ny, nz), f32),
            pltpu.VMEM((2, nf, 4, ny, nz), f32),
            pltpu.VMEM((n_ch, 2, nf, nx, 4, LANES), f32),
            pltpu.VMEM((n_ch, 2, nf, nx, 4, LANES), f32),
            pltpu.VMEM((n_p, nf, nx, ROWS, LANES), f32),
            pltpu.VMEM((n_p, nf, nx, ROWS, LANES), f32),
            pltpu.VMEM((n_p, nf, nx, ROWS, LANES), f32),
            pltpu.VMEM((n_p, 2, nf, 2, ROWS, LANES), f32),
            pltpu.VMEM((n_p, 2, nf, ROWS, LANES), f32),
            pltpu.VMEM((n_p, 2, nf, ROWS, LANES), f32),
            pltpu.VMEM((n_p, nf, ROWS, LANES), f32),
            pltpu.VMEM((n_p, zs - 1, nf, ROWS, LANES), f32),
            pltpu.VMEM((n_p, 2, nf, ROWS, LANES), f32),
            pltpu.VMEM((n_p, nf, ROWS, LANES), f32),
            dma((2, nf)),
            dma((2, nf)),
            dma((n_ch, 2, nf)),
            dma((n_ch, 2, nf)),
            dma((n_p, 2)),
            dma((n_p, 2)),
            dma((n_p,)),
            dma((n_p,)),
            dma((n_p, zs - 1)),
            dma((n_p, zs - 1)),
            dma((n_p,)),
            dma((n_p,)),
            dma((2 * nf,)),
            pltpu.VMEM((nz, nz), jnp.bfloat16),
            pltpu.VMEM((n_products, nx * ny, nz), jnp.bfloat16),
            pltpu.VMEM((n_products, nx * ny, nz), jnp.bfloat16),
            pltpu.VMEM((n_products, nx * ny, nz), f32),
            pltpu.VMEM((6, n_ch, nx * ny, LANES), f32),
            pltpu.VMEM((nf, n_ch, nx * ny, LANES), f32),
        ],
        compiler_params=pltpu.CompilerParams(
            collective_id=0, has_side_effects=True, vmem_limit_bytes=vmem_limit
        ),
    )(state, register)


def solution(mesh):
    spec = P(None, "gx", "yz", None)
    run = functools.partial(body, mesh.shape["gx"], mesh.shape["yz"])
    return jax.shard_map(
        lambda state, register: tuple(run(state, register)),
        mesh=mesh,
        in_specs=(spec, spec),
        out_specs=(spec, spec),
        check_vma=False,
    )
```

```python
import functools

import jax
import jax.numpy as jnp
from jax import lax
from jax.experimental import pallas as pl
from jax.experimental.pallas import tpu as pltpu
from jax.sharding import PartitionSpec as P

gamma_gas = 1.4
central_weights = (4.0 / 5.0, -1.0 / 5.0, 4.0 / 105.0, -1.0 / 280.0)
filter_alpha = 0.49
register_decay = -5.0 / 9.0
register_gain = 15.0 / 16.0
time_step = 0.2
MESH = pl.DeviceIdType.MESH
LANES = 128
ROWS = 8
n_products = 18
vmem_limit = 51 * 1024 * 1024


def filter_constants():
    alpha = filter_alpha
    a0 = (11.0 + 10.0 * alpha) / 16.0
    a1 = (15.0 + 34.0 * alpha) / 32.0
    a2 = (-3.0 + 6.0 * alpha) / 16.0
    a3 = (1.0 - 2.0 * alpha) / 32.0
    q2 = 4.0 * a3 / (2.0 * alpha)
    q1 = (2.0 * a2 - q2) / (2.0 * alpha)
    q0 = (a1 - 3.0 * a3 - q1) / (2.0 * alpha)
    rest = a0 - a2 - q0
    mu = (-1.0 + (1.0 - 4.0 * alpha * alpha) ** 0.5) / (2.0 * alpha)
    kappa = (1.0 + mu * mu) / (1.0 - mu * mu)
    return (q0 + 0.5 * q2, 0.5 * q1, 0.25 * q2), kappa * rest, mu


def split_products(fields):
    density, mom_x, mom_y, mom_z, energy = fields
    inverse = 1.0 / density
    u, v, w = mom_x * inverse, mom_y * inverse, mom_z * inverse
    pressure = (gamma_gas - 1.0) * (energy - 0.5 * (mom_x * u + mom_y * v + mom_z * w))
    total = energy + pressure
    h = total * inverse
    prims = [density, 0.5 * u, 0.5 * v, 0.5 * w, pressure, 0.5 * h]
    return prims, [
        density, w, mom_z,
        mom_z * u, w * u, mom_x, u,
        mom_z * v, w * v, mom_y, v,
        mom_z * w, w * w,
        mom_z * h, w * h, total, h,
        pressure,
    ]


def split_residual(prims, d, scale):
    density, u, v, w, _, h = prims
    u, v, w, h = u + u, v + v, w + w, h + h
    mom = density * w
    mass = d[2] + density * d[1] + w * d[0]

    def moment(q, d_mq, d_wq, d_rq, d_q):
        return scale * (d_mq + density * d_wq + w * d_rq + q * mass + mom * d_q)

    return [
        (2.0 * scale) * mass,
        moment(u, d[3], d[4], d[5], d[6]),
        moment(v, d[7], d[8], d[9], d[10]),
        moment(w, d[11], d[12], d[2], d[1]) + (4.0 * scale) * d[17],
        moment(h, d[13], d[14], d[15], d[16]),
    ]


def primitives(fields):
    density = fields[0]
    inverse = 1.0 / density
    speeds = [fields[i] * inverse for i in (1, 2, 3)]
    kinetic = 0.5 * (
        fields[1] * speeds[0] + fields[2] * speeds[1] + fields[3] * speeds[2]
    )
    pressure = (gamma_gas - 1.0) * (fields[4] - kinetic)
    enthalpy = (fields[4] + pressure) * (0.5 * inverse)
    return [density] + [0.5 * speed for speed in speeds] + [pressure, enthalpy]


def pair_flux(left, right, direction, weight):
    density, speed_x, speed_y, speed_z, pressure, enthalpy = [
        one + other for one, other in zip(left, right)
    ]
    normal = (speed_x, speed_y, speed_z)[direction]
    mass = (weight * density) * normal
    moment = [mass * speed_x, mass * speed_y, mass * speed_z]
    moment[direction] = moment[direction] + weight * pressure
    return [mass] + moment + [mass * enthalpy]


def line_pass(low, high, first, last, direction, weights, get, put):
    held, totals = {}, {}
    for a in range(low, last):
        for b in range(a, min(a + 5, high)):
            if b not in held:
                held[b] = get(b)
        for l in range(1, 5):
            b = a + l
            if b >= high or (a < first and not first <= b < last):
                continue
            flux = pair_flux(held[a], held[b], direction, weights[l - 1])
            if a >= first:
                totals[a] = [t + v for t, v in zip(totals[a], flux)] if a in totals else flux
            if first <= b < last:
                totals[b] = (
                    [t - v for t, v in zip(totals[b], flux)]
                    if b in totals
                    else [-v for v in flux]
                )
        if a >= first:
            put(a, totals.pop(a))
        held.pop(a)


def kernel(
    n_gx,
    n_yz,
    state_in,
    register_in,
    reg_out,
    filt_out,
    state,
    register,
    prims,
    acc,
    xrecv,
    ysend,
    yrecv,
    sec,
    early,
    filt,
    srecv,
    ab,
    pab,
    chip,
    chips,
    inc,
    pinc,
    xs,
    xr,
    ys,
    yr,
    ss,
    sr,
    abs_,
    abr,
    cs,
    cr,
    ins,
    inr,
    local,
    matrix,
    high,
    rest,
    deriv,
    yprims,
    yacc,
):
    nf, nx, ny, nz = state.shape
    n_ch = nz // LANES
    tiles = ny // ROWS
    zs = n_gx // 2
    me = lax.axis_index("gx")
    mine = lax.axis_index("yz")
    core = lax.rem(me, 2)
    chip_at = lax.div(me, 2)
    nxt = lax.rem(me + 1, n_gx)
    prv = lax.rem(me + n_gx - 1, n_gx)
    partner = me + 1 - 2 * core
    ynxt = lax.rem(mine + 1, n_yz)
    yprv = lax.rem(mine + n_yz - 1, n_yz)

    def chip_peer(d):
        return 2 * lax.rem(chip_at + (1 - 2 * core) * d + zs, zs) + core

    barrier = pltpu.get_barrier_semaphore()
    peers = [(prv, mine), (nxt, mine), (me, yprv), (me, ynxt)]
    peers += [(chip_peer(d), mine) for d in range(1, zs)]
    for peer in peers:
        pl.semaphore_signal(barrier, inc=1, device_id=peer, device_id_type=MESH)

    loads = [
        pltpu.make_async_copy(state_in.at[f], state.at[f], local.at[f]) for f in range(nf)
    ]
    loads += [
        pltpu.make_async_copy(register_in.at[f], register.at[f], local.at[nf + f])
        for f in range(nf)
    ]
    for load in loads[:nf]:
        load.start()

    def remote(src, dst, send, recv, peer):
        return pltpu.make_async_remote_copy(
            src_ref=src,
            dst_ref=dst,
            send_sem=send,
            recv_sem=recv,
            device_id=peer,
            device_id_type=MESH,
        )

    def y_copies(ch):
        return [
            remote(
                ysend.at[ch, side, f],
                yrecv.at[ch, side, f],
                ys.at[ch, side, f],
                yr.at[ch, side, f],
                (me, (yprv, ynxt)[side]),
            )
            for f in range(nf)
            for side in range(2)
        ]

    ycopies = [y_copies(ch) for ch in range(n_ch)]
    xcopies = [
        remote(
            state.at[f, pl.ds((0, nx - 4)[side], 4)],
            xrecv.at[side, f],
            xs.at[side, f],
            xr.at[side, f],
            ((prv, nxt)[side], mine),
        )
        for f in range(nf)
        for side in range(2)
    ]
    pl.semaphore_wait(barrier, len(peers))
    for f in range(nf):
        loads[f].wait()

        @pl.loop(0, nx, unroll=4)
        def _(x, f=f):
            for ch in range(n_ch):
                cols = pl.ds(ch * LANES, LANES)
                ysend[ch, 0, f, x] = state[f, x, pl.ds(0, ROWS), cols][:4]
                ysend[ch, 1, f, x] = state[f, x, pl.ds(ny - ROWS, ROWS), cols][4:]

        for k in (2 * f, 2 * f + 1):
            ycopies[0][k].start()
            xcopies[k].start()
    for ch in range(1, n_ch):
        for copy in ycopies[ch]:
            copy.start()
    for load in loads[nf:]:
        load.start()

    gap = lax.broadcasted_iota(jnp.int32, (nz, nz), 0) - lax.broadcasted_iota(
        jnp.int32, (nz, nz), 1
    )
    gap = jnp.where(gap < 0, gap + nz, gap)
    entries = jnp.zeros((nz, nz), jnp.float32)
    for l in range(1, 5):
        whole = float(round(840.0 * central_weights[l - 1]))
        entries = jnp.where(gap == l, whole, jnp.where(gap == nz - l, -whole, entries))
    matrix[...] = entries.astype(jnp.bfloat16)

    weights = [-time_step * w for w in central_weights]

    @pl.loop(0, nx)
    def _(x):
        rows = pl.ds(pl.multiple_of(x * ny, ny), ny)
        own, products = split_products([state[f, x] for f in range(nf)])
        for f in range(6):
            prims[f, x + 4] = own[f]
            for ch in range(n_ch):
                yprims[f, ch, rows, :] = own[f][:, ch * LANES : (ch + 1) * LANES]
        for k, value in enumerate(products):
            part = value.astype(jnp.bfloat16)
            high[k, rows, :] = part
            rest[k, rows, :] = (value - part.astype(jnp.float32)).astype(jnp.bfloat16)

    @pl.loop(0, n_products)
    def _(k):
        whole = jnp.dot(high[k], matrix[...], preferred_element_type=jnp.float32)
        deriv[k] = whole + jnp.dot(rest[k], matrix[...], preferred_element_type=jnp.float32)

    @pl.loop(0, nx * tiles)
    def _(i):
        x = i // tiles
        rows = pl.ds(pl.multiple_of((i % tiles) * ROWS, ROWS), ROWS)
        flat = pl.ds(pl.multiple_of(i * ROWS, ROWS), ROWS)
        total = split_residual(
            [prims[f, x + 4, rows, :] for f in range(6)],
            [deriv[k, flat, :] for k in range(n_products)],
            -time_step / (4.0 * 840.0),
        )
        for f in range(nf):
            acc[f, x, rows, :] = total[f]

    @pl.loop(0, n_ch * (nx // ROWS))
    def _(i):
        ch = i // (nx // ROWS)
        base = (i % (nx // ROWS)) * (ROWS * ny)

        def at(y):
            return pl.ds(base + y, ROWS, stride=ny)

        line_pass(
            0,
            ny,
            0,
            ny,
            1,
            weights,
            lambda y: [yprims[f, ch, at(y), :] for f in range(6)],
            lambda y, total: [
                yacc.__setitem__((f, ch, at(y), slice(None)), total[f]) for f in range(nf)
            ],
        )

    for copy in xcopies:
        copy.wait_recv()

    @pl.loop(0, 4 * tiles)
    def _(i):
        x = i // tiles
        rows = pl.ds(pl.multiple_of((i % tiles) * ROWS, ROWS), ROWS)
        for side in range(2):
            got = primitives([xrecv[side, f, x, rows, :] for f in range(nf)])
            for f in range(6):
                prims[f, x + (nx + 4, 0)[side], rows, :] = got[f]

    for load in loads[nf:]:
        load.wait()

    stencil, remainder, mu = filter_constants()
    rho = mu**nx
    low = lax.broadcasted_iota(jnp.int32, (ROWS, LANES), 0) < 4
    top, bottom = pl.ds(0, ROWS), pl.ds(ny - ROWS, ROWS)

    def inner(first, last):
        return jnp.where(low, last, first)

    def outer(first, last):
        return jnp.where(low, first, last)

    def x_pass(ch):
        cols = pl.ds(ch * LANES, LANES)

        @pl.loop(0, tiles)
        def _(i):
            rows = pl.ds(pl.multiple_of(i * ROWS, ROWS), ROWS)

            def put(x, total):
                for f in range(nf):
                    acc[f, x, rows, cols] = acc[f, x, rows, cols] + total[f]

            line_pass(
                -4,
                nx + 4,
                0,
                nx,
                0,
                weights,
                lambda x: [prims[f, x + 4, rows, cols] for f in range(6)],
                put,
            )

        @pl.loop(0, nx, unroll=2)
        def _(x):
            for f in range(nf):
                ends = []
                for k, rows in enumerate((top, bottom)):
                    flat = pl.ds(pl.multiple_of(x * ny + k * (ny - ROWS), ROWS), ROWS)
                    ends.append(
                        register_decay * register[f, x, rows, cols]
                        + (acc[f, x, rows, cols] + yacc[f, ch, flat, :])
                    )
                first, last = ends
                state_first, state_last = state[f, x, top, cols], state[f, x, bottom, cols]
                for piece, pick in ((ch, inner), (n_ch + ch, outer)):
                    value = pick(first, last)
                    early[piece, f, x] = value
                    sec[piece, f, x] = pick(state_first, state_last) + register_gain * value

    signs = []
    spot = lax.broadcasted_iota(jnp.int32, (ROWS, LANES), 0)
    for l in range(1, 5):
        w = weights[l - 1]
        signs.append(jnp.where(spot < l, -w, jnp.where(spot >= ROWS - l, w, 0.0)))

    def y_pass(ch):
        piece = n_ch + ch
        cols = pl.ds(ch * LANES, LANES)
        for copy in ycopies[ch]:
            copy.wait_recv()

        @pl.loop(0, nx, unroll=2)
        def _(x):
            halo = primitives(
                [
                    jnp.concatenate([yrecv[ch, 0, f, x], yrecv[ch, 1, f, x]], axis=0)
                    for f in range(nf)
                ]
            )
            own = [
                outer(prims[f, x + 4, top, cols], prims[f, x + 4, bottom, cols])
                for f in range(6)
            ]
            total = [jnp.zeros((ROWS, LANES), jnp.float32) for _ in range(nf)]
            for l in range(1, 5):
                across = [
                    jnp.where(low, pltpu.roll(q, l, axis=0), pltpu.roll(q, ROWS - l, axis=0))
                    if l < 4
                    else pltpu.roll(q, l, axis=0)
                    for q in halo
                ]
                flux = pair_flux(own, across, 1, signs[l - 1])
                total = [t + v for t, v in zip(total, flux)]
            for f in range(nf):
                new = early[piece, f, x] + total[f]
                sec[piece, f, x] = sec[piece, f, x] + register_gain * total[f]
                mid = early[ch, f, x]
                reg_out[f, x, top, cols] = jnp.where(low, new, mid)
                reg_out[f, x, bottom, cols] = jnp.where(low, mid, new)

    def section_copies(p):
        return [
            remote(
                sec.at[p, :, pl.ds(0, 2)],
                srecv.at[p, 0],
                ss.at[p, 0],
                sr.at[p, 0],
                (prv, mine),
            ),
            remote(
                sec.at[p, :, pl.ds(nx - 2, 2)],
                srecv.at[p, 1],
                ss.at[p, 1],
                sr.at[p, 1],
                (nxt, mine),
            ),
        ]

    def chip_copies(p):
        return [
            remote(
                chip.at[p],
                chips.at[p, d - 1],
                cs.at[p, d - 1],
                cr.at[p, d - 1],
                (chip_peer(d), mine),
            )
            for d in range(1, zs)
        ]

    pieces = range(2 * n_ch)
    scopies = [section_copies(p) for p in pieces]
    abcopies = [
        remote(ab.at[p], pab.at[p], abs_.at[p], abr.at[p], (partner, mine)) for p in pieces
    ]
    ccopies = [chip_copies(p) for p in pieces]
    icopies = [
        remote(inc.at[p, core], pinc.at[p], ins.at[p], inr.at[p], (partner, mine))
        for p in pieces
    ]

    def begin(p):
        for f in range(nf):
            ahead = sec[p, f, 0]
            back = sec[p, f, nx - 1]
            for j in range(1, nx):
                ahead = sec[p, f, j] + mu * ahead
                back = sec[p, f, nx - 1 - j] + mu * back
            ab[p, 0, f] = ahead
            ab[p, 1, f] = back
        abcopies[p].start()
        for copy in scopies[p]:
            copy.start()

    def across_chips(p):
        abcopies[p].wait_recv()
        for f in range(nf):
            chip[p, f] = pab[p, core, f] + rho * ab[p, core, f]
        for copy in ccopies[p]:
            copy.start()

    def incoming(p):
        for copy in ccopies[p]:
            copy.wait_recv()
        scale = 1.0 / (1.0 - rho ** (2 * zs))
        for f in range(nf):
            total = (scale * rho ** (2 * (zs - 1))) * chip[p, f]
            for d in range(1, zs):
                total = total + (scale * rho ** (2 * (d - 1))) * chips[p, d - 1, f]
            inc[p, core, f] = total
        icopies[p].start()

    def finish(p):
        for copy in scopies[p]:
            copy.wait()
        icopies[p].wait()
        for f in range(nf):
            inc[p, 1 - core, f] = pab[p, 1 - core, f] + rho * pinc[p, f]
        for f in range(nf):
            s = (
                [srecv[p, 1, f, 0], srecv[p, 1, f, 1]]
                + [sec[p, f, j] for j in range(nx)]
                + [srecv[p, 0, f, 0], srecv[p, 0, f, 1]]
            )
            left = inc[p, 0, f]
            for j in range(nx):
                left = s[j + 2] + mu * left
                near = (
                    stencil[0] * s[j + 2]
                    + stencil[1] * (s[j + 1] + s[j + 3])
                    + stencil[2] * (s[j] + s[j + 4])
                )
                filt[p, f, j] = near + remainder * left
            right = inc[p, 1, f]
            for j in reversed(range(nx)):
                value = filt[p, f, j] + (remainder * mu) * right
                if p < n_ch:
                    filt[p, f, j] = value
                else:
                    mid = filt[p - n_ch, f, j]
                    cols = pl.ds((p - n_ch) * LANES, LANES)
                    filt_out[f, j, top, cols] = jnp.where(low, value, mid)
                    filt_out[f, j, bottom, cols] = jnp.where(low, mid, value)
                right = s[j + 2] + mu * right

    chunks = range(n_ch)

    for ch in chunks:
        x_pass(ch)
        begin(ch)
    for ch in chunks:
        across_chips(ch)
    for ch in chunks:
        y_pass(ch)
        begin(n_ch + ch)
        if ch == 0:
            for early_piece in chunks:
                incoming(early_piece)
        else:
            incoming(n_ch + ch - 1)
        across_chips(n_ch + ch)
    for p in range(2 * n_ch - 1):
        finish(p)
    incoming(2 * n_ch - 1)
    finish(2 * n_ch - 1)

    for ch in chunks:
        for copy in ycopies[ch]:
            copy.wait_send()
    for p in pieces:
        abcopies[p].wait_send()
        for copy in ccopies[p]:
            copy.wait_send()
    for copy in xcopies:
        copy.wait_send()


def hand_out(first, second, out_first, out_second, sems):
    copies = []
    for k, (src, dst) in enumerate(((first, out_first), (second, out_second))):
        for f in range(src.shape[0]):
            copies.append(pltpu.make_async_copy(src.at[f], dst.at[f], sems.at[k, f]))
    for copy in copies:
        copy.start()
    for copy in copies:
        copy.wait()


def body(n_gx, n_yz, state, register):
    nf, nx, ny, nz = state.shape
    n_ch = nz // LANES
    n_p = 2 * n_ch
    zs = n_gx // 2
    f32 = jnp.float32
    dma = pltpu.SemaphoreType.DMA
    results = pl.pallas_call(
        functools.partial(kernel, n_gx, n_yz),
        out_shape=[jax.ShapeDtypeStruct(state.shape, f32)] * 2,
        in_specs=[pl.BlockSpec(memory_space=pl.ANY)] * 2,
        out_specs=[pl.BlockSpec(memory_space=pltpu.VMEM)] * 2,
        scratch_shapes=[
            pltpu.VMEM((nf, nx, ny, nz), f32),
            pltpu.VMEM((nf, nx, ny, nz), f32),
            pltpu.VMEM((6, nx + 8, ny, nz), f32),
            pltpu.VMEM((nf, nx, ny, nz), f32),
            pltpu.VMEM((2, nf, 4, ny, nz), f32),
            pltpu.VMEM((n_ch, 2, nf, nx, 4, LANES), f32),
            pltpu.VMEM((n_ch, 2, nf, nx, 4, LANES), f32),
            pltpu.VMEM((n_p, nf, nx, ROWS, LANES), f32),
            pltpu.VMEM((n_p, nf, nx, ROWS, LANES), f32),
            pltpu.VMEM((n_p, nf, nx, ROWS, LANES), f32),
            pltpu.VMEM((n_p, 2, nf, 2, ROWS, LANES), f32),
            pltpu.VMEM((n_p, 2, nf, ROWS, LANES), f32),
            pltpu.VMEM((n_p, 2, nf, ROWS, LANES), f32),
            pltpu.VMEM((n_p, nf, ROWS, LANES), f32),
            pltpu.VMEM((n_p, zs - 1, nf, ROWS, LANES), f32),
            pltpu.VMEM((n_p, 2, nf, ROWS, LANES), f32),
            pltpu.VMEM((n_p, nf, ROWS, LANES), f32),
            dma((2, nf)),
            dma((2, nf)),
            dma((n_ch, 2, nf)),
            dma((n_ch, 2, nf)),
            dma((n_p, 2)),
            dma((n_p, 2)),
            dma((n_p,)),
            dma((n_p,)),
            dma((n_p, zs - 1)),
            dma((n_p, zs - 1)),
            dma((n_p,)),
            dma((n_p,)),
            dma((2 * nf,)),
            pltpu.VMEM((nz, nz), jnp.bfloat16),
            pltpu.VMEM((n_products, nx * ny, nz), jnp.bfloat16),
            pltpu.VMEM((n_products, nx * ny, nz), jnp.bfloat16),
            pltpu.VMEM((n_products, nx * ny, nz), f32),
            pltpu.VMEM((6, n_ch, nx * ny, LANES), f32),
            pltpu.VMEM((nf, n_ch, nx * ny, LANES), f32),
        ],
        compiler_params=pltpu.CompilerParams(
            collective_id=0, has_side_effects=True, vmem_limit_bytes=vmem_limit
        ),
    )(state, register)
    return pl.pallas_call(
        hand_out,
        out_shape=[jax.ShapeDtypeStruct(state.shape, f32)] * 2,
        in_specs=[pl.BlockSpec(memory_space=pltpu.VMEM)] * 2,
        out_specs=[pl.BlockSpec(memory_space=pl.ANY)] * 2,
        scratch_shapes=[dma((2, nf))],
    )(*results)


def solution(mesh):
    spec = P(None, "gx", "yz", None)
    run = functools.partial(body, mesh.shape["gx"], mesh.shape["yz"])
    return jax.shard_map(
        lambda state, register: tuple(run(state, register)),
        mesh=mesh,
        in_specs=(spec, spec),
        out_specs=(spec, spec),
        check_vma=False,
    )
```

```python
import functools

import jax
import jax.numpy as jnp
from jax import lax
from jax.experimental import pallas as pl
from jax.experimental.pallas import tpu as pltpu
from jax.sharding import PartitionSpec as P

gamma_gas = 1.4
central_weights = (4.0 / 5.0, -1.0 / 5.0, 4.0 / 105.0, -1.0 / 280.0)
filter_alpha = 0.49
register_decay = -5.0 / 9.0
register_gain = 15.0 / 16.0
time_step = 0.2
MESH = pl.DeviceIdType.MESH
LANES = 128
ROWS = 8
n_products = 18
vmem_limit = 51 * 1024 * 1024


def filter_constants():
    alpha = filter_alpha
    a0 = (11.0 + 10.0 * alpha) / 16.0
    a1 = (15.0 + 34.0 * alpha) / 32.0
    a2 = (-3.0 + 6.0 * alpha) / 16.0
    a3 = (1.0 - 2.0 * alpha) / 32.0
    q2 = 4.0 * a3 / (2.0 * alpha)
    q1 = (2.0 * a2 - q2) / (2.0 * alpha)
    q0 = (a1 - 3.0 * a3 - q1) / (2.0 * alpha)
    rest = a0 - a2 - q0
    mu = (-1.0 + (1.0 - 4.0 * alpha * alpha) ** 0.5) / (2.0 * alpha)
    kappa = (1.0 + mu * mu) / (1.0 - mu * mu)
    return (q0 + 0.5 * q2, 0.5 * q1, 0.25 * q2), kappa * rest, mu


def split_products(fields):
    density, mom_x, mom_y, mom_z, energy = fields
    inverse = 1.0 / density
    u, v, w = mom_x * inverse, mom_y * inverse, mom_z * inverse
    pressure = (gamma_gas - 1.0) * (energy - 0.5 * (mom_x * u + mom_y * v + mom_z * w))
    total = energy + pressure
    h = total * inverse
    prims = [density, 0.5 * u, 0.5 * v, 0.5 * w, pressure, 0.5 * h]
    return prims, [
        density, w, mom_z,
        mom_z * u, w * u, mom_x, u,
        mom_z * v, w * v, mom_y, v,
        mom_z * w, w * w,
        mom_z * h, w * h, total, h,
        pressure,
    ]


def split_residual(prims, d, scale):
    density, u, v, w, _, h = prims
    u, v, w, h = u + u, v + v, w + w, h + h
    mom = density * w
    mass = d[2] + density * d[1] + w * d[0]

    def moment(q, d_mq, d_wq, d_rq, d_q):
        return scale * (d_mq + density * d_wq + w * d_rq + q * mass + mom * d_q)

    return [
        (2.0 * scale) * mass,
        moment(u, d[3], d[4], d[5], d[6]),
        moment(v, d[7], d[8], d[9], d[10]),
        moment(w, d[11], d[12], d[2], d[1]) + (4.0 * scale) * d[17],
        moment(h, d[13], d[14], d[15], d[16]),
    ]


def primitives(fields):
    density = fields[0]
    inverse = 1.0 / density
    speeds = [fields[i] * inverse for i in (1, 2, 3)]
    kinetic = 0.5 * (
        fields[1] * speeds[0] + fields[2] * speeds[1] + fields[3] * speeds[2]
    )
    pressure = (gamma_gas - 1.0) * (fields[4] - kinetic)
    enthalpy = (fields[4] + pressure) * (0.5 * inverse)
    return [density] + [0.5 * speed for speed in speeds] + [pressure, enthalpy]


def pair_flux(left, right, direction, weight):
    density, speed_x, speed_y, speed_z, pressure, enthalpy = [
        one + other for one, other in zip(left, right)
    ]
    normal = (speed_x, speed_y, speed_z)[direction]
    mass = (weight * density) * normal
    moment = [mass * speed_x, mass * speed_y, mass * speed_z]
    moment[direction] = moment[direction] + weight * pressure
    return [mass] + moment + [mass * enthalpy]


def line_pass(low, high, first, last, direction, weights, get, put):
    held, totals = {}, {}
    for a in range(low, last):
        for b in range(a, min(a + 5, high)):
            if b not in held:
                held[b] = get(b)
        for l in range(1, 5):
            b = a + l
            if b >= high or (a < first and not first <= b < last):
                continue
            flux = pair_flux(held[a], held[b], direction, weights[l - 1])
            if a >= first:
                totals[a] = [t + v for t, v in zip(totals[a], flux)] if a in totals else flux
            if first <= b < last:
                totals[b] = (
                    [t - v for t, v in zip(totals[b], flux)]
                    if b in totals
                    else [-v for v in flux]
                )
        if a >= first:
            put(a, totals.pop(a))
        held.pop(a)


def kernel(
    n_gx,
    n_yz,
    state_in,
    register_in,
    reg_out,
    filt_out,
    state,
    register,
    prims,
    acc,
    xrecv,
    ysend,
    yrecv,
    sec,
    early,
    filt,
    srecv,
    ab,
    pab,
    chip,
    chips,
    inc,
    pinc,
    xs,
    xr,
    ys,
    yr,
    ss,
    sr,
    abs_,
    abr,
    cs,
    cr,
    ins,
    inr,
    local,
    matrix,
    high,
    rest,
    deriv,
    yprims,
    yacc,
):
    nf, nx, ny, nz = state.shape
    n_ch = nz // LANES
    tiles = ny // ROWS
    zs = n_gx // 2
    me = lax.axis_index("gx")
    mine = lax.axis_index("yz")
    core = lax.rem(me, 2)
    chip_at = lax.div(me, 2)
    nxt = lax.rem(me + 1, n_gx)
    prv = lax.rem(me + n_gx - 1, n_gx)
    partner = me + 1 - 2 * core
    ynxt = lax.rem(mine + 1, n_yz)
    yprv = lax.rem(mine + n_yz - 1, n_yz)

    def chip_peer(d):
        return 2 * lax.rem(chip_at + (1 - 2 * core) * d + zs, zs) + core

    barrier = pltpu.get_barrier_semaphore()
    peers = [(prv, mine), (nxt, mine), (me, yprv), (me, ynxt)]
    peers += [(chip_peer(d), mine) for d in range(1, zs)]
    for peer in peers:
        pl.semaphore_signal(barrier, inc=1, device_id=peer, device_id_type=MESH)

    loads = [
        pltpu.make_async_copy(state_in.at[f], state.at[f], local.at[f]) for f in range(nf)
    ]
    loads += [
        pltpu.make_async_copy(register_in.at[f], register.at[f], local.at[nf + f])
        for f in range(nf)
    ]
    for load in loads[:nf]:
        load.start()

    def remote(src, dst, send, recv, peer):
        return pltpu.make_async_remote_copy(
            src_ref=src,
            dst_ref=dst,
            send_sem=send,
            recv_sem=recv,
            device_id=peer,
            device_id_type=MESH,
        )

    def y_copies(ch):
        return [
            remote(
                ysend.at[ch, side, f],
                yrecv.at[ch, side, f],
                ys.at[ch, side, f],
                yr.at[ch, side, f],
                (me, (yprv, ynxt)[side]),
            )
            for f in range(nf)
            for side in range(2)
        ]

    ycopies = [y_copies(ch) for ch in range(n_ch)]
    xcopies = [
        remote(
            state.at[f, pl.ds((0, nx - 4)[side], 4)],
            xrecv.at[side, f],
            xs.at[side, f],
            xr.at[side, f],
            ((prv, nxt)[side], mine),
        )
        for f in range(nf)
        for side in range(2)
    ]
    pl.semaphore_wait(barrier, len(peers))
    for f in range(nf):
        loads[f].wait()

        @pl.loop(0, nx, unroll=4)
        def _(x, f=f):
            for ch in range(n_ch):
                cols = pl.ds(ch * LANES, LANES)
                ysend[ch, 0, f, x] = state[f, x, pl.ds(0, ROWS), cols][:4]
                ysend[ch, 1, f, x] = state[f, x, pl.ds(ny - ROWS, ROWS), cols][4:]

        for k in (2 * f, 2 * f + 1):
            ycopies[0][k].start()
            xcopies[k].start()
    for ch in range(1, n_ch):
        for copy in ycopies[ch]:
            copy.start()
    for load in loads[nf:]:
        load.start()

    gap = lax.broadcasted_iota(jnp.int32, (nz, nz), 0) - lax.broadcasted_iota(
        jnp.int32, (nz, nz), 1
    )
    gap = jnp.where(gap < 0, gap + nz, gap)
    entries = jnp.zeros((nz, nz), jnp.float32)
    for l in range(1, 5):
        whole = float(round(840.0 * central_weights[l - 1]))
        entries = jnp.where(gap == l, whole, jnp.where(gap == nz - l, -whole, entries))
    matrix[...] = entries.astype(jnp.bfloat16)

    weights = [-time_step * w for w in central_weights]

    @pl.loop(0, nx)
    def _(x):
        rows = pl.ds(pl.multiple_of(x * ny, ny), ny)
        own, products = split_products([state[f, x] for f in range(nf)])
        for f in range(6):
            prims[f, x + 4] = own[f]
            for ch in range(n_ch):
                yprims[f, ch, rows, :] = own[f][:, ch * LANES : (ch + 1) * LANES]
        for k, value in enumerate(products):
            part = value.astype(jnp.bfloat16)
            high[k, rows, :] = part
            rest[k, rows, :] = (value - part.astype(jnp.float32)).astype(jnp.bfloat16)

    @pl.loop(0, n_products)
    def _(k):
        whole = jnp.dot(high[k], matrix[...], preferred_element_type=jnp.float32)
        deriv[k] = whole + jnp.dot(rest[k], matrix[...], preferred_element_type=jnp.float32)

    @pl.loop(0, nx * tiles)
    def _(i):
        x = i // tiles
        rows = pl.ds(pl.multiple_of((i % tiles) * ROWS, ROWS), ROWS)
        flat = pl.ds(pl.multiple_of(i * ROWS, ROWS), ROWS)
        total = split_residual(
            [prims[f, x + 4, rows, :] for f in range(6)],
            [deriv[k, flat, :] for k in range(n_products)],
            -time_step / (4.0 * 840.0),
        )
        for f in range(nf):
            acc[f, x, rows, :] = total[f]

    @pl.loop(0, n_ch * (nx // ROWS))
    def _(i):
        ch = i // (nx // ROWS)
        base = (i % (nx // ROWS)) * (ROWS * ny)

        def at(y):
            return pl.ds(base + y, ROWS, stride=ny)

        line_pass(
            0,
            ny,
            0,
            ny,
            1,
            weights,
            lambda y: [yprims[f, ch, at(y), :] for f in range(6)],
            lambda y, total: [
                yacc.__setitem__((f, ch, at(y), slice(None)), total[f]) for f in range(nf)
            ],
        )

    for copy in xcopies:
        copy.wait_recv()

    @pl.loop(0, 4 * tiles)
    def _(i):
        x = i // tiles
        rows = pl.ds(pl.multiple_of((i % tiles) * ROWS, ROWS), ROWS)
        for side in range(2):
            got = primitives([xrecv[side, f, x, rows, :] for f in range(nf)])
            for f in range(6):
                prims[f, x + (nx + 4, 0)[side], rows, :] = got[f]

    for load in loads[nf:]:
        load.wait()

    stencil, remainder, mu = filter_constants()
    rho = mu**nx
    low = lax.broadcasted_iota(jnp.int32, (ROWS, LANES), 0) < 4
    top, bottom = pl.ds(0, ROWS), pl.ds(ny - ROWS, ROWS)

    def inner(first, last):
        return jnp.where(low, last, first)

    def outer(first, last):
        return jnp.where(low, first, last)

    def x_pass(ch):
        cols = pl.ds(ch * LANES, LANES)

        @pl.loop(0, tiles)
        def _(i):
            rows = pl.ds(pl.multiple_of(i * ROWS, ROWS), ROWS)

            def put(x, total):
                for f in range(nf):
                    acc[f, x, rows, cols] = acc[f, x, rows, cols] + total[f]

            line_pass(
                -4,
                nx + 4,
                0,
                nx,
                0,
                weights,
                lambda x: [prims[f, x + 4, rows, cols] for f in range(6)],
                put,
            )

        @pl.loop(0, nx, unroll=2)
        def _(x):
            for f in range(nf):
                ends = []
                for k, rows in enumerate((top, bottom)):
                    flat = pl.ds(pl.multiple_of(x * ny + k * (ny - ROWS), ROWS), ROWS)
                    ends.append(
                        register_decay * register[f, x, rows, cols]
                        + (acc[f, x, rows, cols] + yacc[f, ch, flat, :])
                    )
                first, last = ends
                state_first, state_last = state[f, x, top, cols], state[f, x, bottom, cols]
                for piece, pick in ((ch, inner), (n_ch + ch, outer)):
                    value = pick(first, last)
                    early[piece, f, x] = value
                    sec[piece, f, x] = pick(state_first, state_last) + register_gain * value

    signs = []
    spot = lax.broadcasted_iota(jnp.int32, (ROWS, LANES), 0)
    for l in range(1, 5):
        w = weights[l - 1]
        signs.append(jnp.where(spot < l, -w, jnp.where(spot >= ROWS - l, w, 0.0)))

    def y_pass(ch):
        piece = n_ch + ch
        cols = pl.ds(ch * LANES, LANES)
        for copy in ycopies[ch]:
            copy.wait_recv()

        @pl.loop(0, nx, unroll=2)
        def _(x):
            halo = primitives(
                [
                    jnp.concatenate([yrecv[ch, 0, f, x], yrecv[ch, 1, f, x]], axis=0)
                    for f in range(nf)
                ]
            )
            own = [
                outer(prims[f, x + 4, top, cols], prims[f, x + 4, bottom, cols])
                for f in range(6)
            ]
            total = [jnp.zeros((ROWS, LANES), jnp.float32) for _ in range(nf)]
            for l in range(1, 5):
                across = [
                    jnp.where(low, pltpu.roll(q, l, axis=0), pltpu.roll(q, ROWS - l, axis=0))
                    if l < 4
                    else pltpu.roll(q, l, axis=0)
                    for q in halo
                ]
                flux = pair_flux(own, across, 1, signs[l - 1])
                total = [t + v for t, v in zip(total, flux)]
            for f in range(nf):
                new = early[piece, f, x] + total[f]
                sec[piece, f, x] = sec[piece, f, x] + register_gain * total[f]
                mid = early[ch, f, x]
                reg_out[f, x, top, cols] = jnp.where(low, new, mid)
                reg_out[f, x, bottom, cols] = jnp.where(low, mid, new)

    def section_copies(p):
        return [
            remote(
                sec.at[p, :, pl.ds(0, 2)],
                srecv.at[p, 0],
                ss.at[p, 0],
                sr.at[p, 0],
                (prv, mine),
            ),
            remote(
                sec.at[p, :, pl.ds(nx - 2, 2)],
                srecv.at[p, 1],
                ss.at[p, 1],
                sr.at[p, 1],
                (nxt, mine),
            ),
        ]

    def chip_copies(p):
        return [
            remote(
                chip.at[p],
                chips.at[p, d - 1],
                cs.at[p, d - 1],
                cr.at[p, d - 1],
                (chip_peer(d), mine),
            )
            for d in range(1, zs)
        ]

    pieces = range(2 * n_ch)
    scopies = [section_copies(p) for p in pieces]
    abcopies = [
        remote(ab.at[p], pab.at[p], abs_.at[p], abr.at[p], (partner, mine)) for p in pieces
    ]
    ccopies = [chip_copies(p) for p in pieces]
    icopies = [
        remote(inc.at[p, core], pinc.at[p], ins.at[p], inr.at[p], (partner, mine))
        for p in pieces
    ]

    def begin(p):
        for f in range(nf):
            ahead = sec[p, f, 0]
            back = sec[p, f, nx - 1]
            for j in range(1, nx):
                ahead = sec[p, f, j] + mu * ahead
                back = sec[p, f, nx - 1 - j] + mu * back
            ab[p, 0, f] = ahead
            ab[p, 1, f] = back
        abcopies[p].start()
        for copy in scopies[p]:
            copy.start()

    def across_chips(p):
        abcopies[p].wait_recv()
        for f in range(nf):
            chip[p, f] = pab[p, core, f] + rho * ab[p, core, f]
        for copy in ccopies[p]:
            copy.start()

    def incoming(p):
        for copy in ccopies[p]:
            copy.wait_recv()
        scale = 1.0 / (1.0 - rho ** (2 * zs))
        for f in range(nf):
            total = (scale * rho ** (2 * (zs - 1))) * chip[p, f]
            for d in range(1, zs):
                total = total + (scale * rho ** (2 * (d - 1))) * chips[p, d - 1, f]
            inc[p, core, f] = total
        icopies[p].start()

    def finish(p):
        for copy in scopies[p]:
            copy.wait()
        icopies[p].wait()
        for f in range(nf):
            inc[p, 1 - core, f] = pab[p, 1 - core, f] + rho * pinc[p, f]
        for f in range(nf):
            s = (
                [srecv[p, 1, f, 0], srecv[p, 1, f, 1]]
                + [sec[p, f, j] for j in range(nx)]
                + [srecv[p, 0, f, 0], srecv[p, 0, f, 1]]
            )
            left = inc[p, 0, f]
            for j in range(nx):
                left = s[j + 2] + mu * left
                near = (
                    stencil[0] * s[j + 2]
                    + stencil[1] * (s[j + 1] + s[j + 3])
                    + stencil[2] * (s[j] + s[j + 4])
                )
                filt[p, f, j] = near + remainder * left
            right = inc[p, 1, f]
            for j in reversed(range(nx)):
                value = filt[p, f, j] + (remainder * mu) * right
                if p < n_ch:
                    filt[p, f, j] = value
                else:
                    mid = filt[p - n_ch, f, j]
                    cols = pl.ds((p - n_ch) * LANES, LANES)
                    filt_out[f, j, top, cols] = jnp.where(low, value, mid)
                    filt_out[f, j, bottom, cols] = jnp.where(low, mid, value)
                right = s[j + 2] + mu * right

    chunks = range(n_ch)

    for ch in chunks:
        x_pass(ch)
        begin(ch)
    for ch in chunks:
        across_chips(ch)
    for ch in chunks:
        y_pass(ch)
        begin(n_ch + ch)
        if ch == 0:
            for early_piece in chunks:
                incoming(early_piece)
        else:
            incoming(n_ch + ch - 1)
        across_chips(n_ch + ch)
    for p in range(2 * n_ch - 1):
        finish(p)
    incoming(2 * n_ch - 1)
    finish(2 * n_ch - 1)

    for ch in chunks:
        for copy in ycopies[ch]:
            copy.wait_send()
    for p in pieces:
        abcopies[p].wait_send()
        for copy in ccopies[p]:
            copy.wait_send()
    for copy in xcopies:
        copy.wait_send()


def body(n_gx, n_yz, state, register):
    nf, nx, ny, nz = state.shape
    n_ch = nz // LANES
    n_p = 2 * n_ch
    zs = n_gx // 2
    f32 = jnp.float32
    dma = pltpu.SemaphoreType.DMA
    return pl.pallas_call(
        functools.partial(kernel, n_gx, n_yz),
        out_shape=[jax.ShapeDtypeStruct(state.shape, f32)] * 2,
        in_specs=[pl.BlockSpec(memory_space=pl.ANY)] * 2,
        out_specs=[pl.BlockSpec(memory_space=pltpu.VMEM)] * 2,
        scratch_shapes=[
            pltpu.VMEM((nf, nx, ny, nz), f32),
            pltpu.VMEM((nf, nx, ny, nz), f32),
            pltpu.VMEM((6, nx + 8, ny, nz), f32),
            pltpu.VMEM((nf, nx, ny, nz), f32),
            pltpu.VMEM((2, nf, 4, ny, nz), f32),
            pltpu.VMEM((n_ch, 2, nf, nx, 4, LANES), f32),
            pltpu.VMEM((n_ch, 2, nf, nx, 4, LANES), f32),
            pltpu.VMEM((n_p, nf, nx, ROWS, LANES), f32),
            pltpu.VMEM((n_p, nf, nx, ROWS, LANES), f32),
            pltpu.VMEM((n_p, nf, nx, ROWS, LANES), f32),
            pltpu.VMEM((n_p, 2, nf, 2, ROWS, LANES), f32),
            pltpu.VMEM((n_p, 2, nf, ROWS, LANES), f32),
            pltpu.VMEM((n_p, 2, nf, ROWS, LANES), f32),
            pltpu.VMEM((n_p, nf, ROWS, LANES), f32),
            pltpu.VMEM((n_p, zs - 1, nf, ROWS, LANES), f32),
            pltpu.VMEM((n_p, 2, nf, ROWS, LANES), f32),
            pltpu.VMEM((n_p, nf, ROWS, LANES), f32),
            dma((2, nf)),
            dma((2, nf)),
            dma((n_ch, 2, nf)),
            dma((n_ch, 2, nf)),
            dma((n_p, 2)),
            dma((n_p, 2)),
            dma((n_p,)),
            dma((n_p,)),
            dma((n_p, zs - 1)),
            dma((n_p, zs - 1)),
            dma((n_p,)),
            dma((n_p,)),
            dma((2 * nf,)),
            pltpu.VMEM((nz, nz), jnp.bfloat16),
            pltpu.VMEM((n_products, nx * ny, nz), jnp.bfloat16),
            pltpu.VMEM((n_products, nx * ny, nz), jnp.bfloat16),
            pltpu.VMEM((n_products, nx * ny, nz), f32),
            pltpu.VMEM((6, n_ch, nx * ny, LANES), f32),
            pltpu.VMEM((nf, n_ch, nx * ny, LANES), f32),
        ],
        compiler_params=pltpu.CompilerParams(
            collective_id=0, has_side_effects=True, vmem_limit_bytes=vmem_limit
        ),
    )(state, register)


def solution(mesh):
    spec = P(None, "gx", "yz", None)
    run = functools.partial(body, mesh.shape["gx"], mesh.shape["yz"])
    return jax.shard_map(
        lambda state, register: tuple(run(state, register)),
        mesh=mesh,
        in_specs=(spec, spec),
        out_specs=(spec, spec),
        check_vma=False,
    )
```
